256 devices in a mesh: seq: 16 (over z, y_lo), dp: 16 (over y_hi, x, core).
Axes of the slice: x: 4, y: 4 (y_hi: 2, y_lo: 2; y = y_hi * 2 + y_lo), z: 8, core: 2. Of those that a mesh axis runs over, the one named last changes fastest.
Arguments:
- hidden_in: bfloat16 [16, 4096, 1152], P('dp', 'seq'), may hold values from -4 to 4
- spatial_qkv: bfloat16 [16, 4096, 3456], P('dp', 'seq'), may hold values from -6 to 6
- temporal_grad: bfloat16 [16, 4096, 1152], P('dp', 'seq'), may hold values from -6 to 6
- pair_grad: bfloat16 [16, 4096, 1152], P('dp', 'seq'), may hold values from -4 to 4
- spatial_proj: bfloat16 [1152, 1152], P('seq'), may hold values from -0.1875 to 0.1875
- temporal_weight: bfloat16 [1152, 3456], P('seq'), may hold values from -0.1875 to 0.1875
Outputs:
- spatial_qkv_grad: bfloat16 [16, 4096, 3456], P('dp', 'seq')
- hidden_grad: bfloat16 [16, 4096, 1152], P('dp', 'seq')
- spatial_proj_grad: bfloat16 [1152, 1152], P('seq')
- temporal_weight_grad: bfloat16 [1152, 3456], P('seq')
The draws below stay inside these ranges and needn't reach their ends.
All inputs are finite; a program needn't handle non-finite values.
Results may differ from the reference program's by a relative error of at most 0.034.
Values may be sent and summed in bfloat16 or wider, within the bound.
No kernel may reach another device: no remote copies, remote signals or barrier semaphores. Data moves between devices by JAX's collectives and lax.ppermute only.
A program may use at most 128 MiB of HBM per device.

```python
import jax
import jax.numpy as jnp
from jax import lax

D = 1152
HEADS = 16
FR_DEV = 1
P_SIZE = 256
QKV = 3456
F = 16
PATCH_DEV = 16
TOKENS = 4096
CLIPS = 16
N_SEQ = 16


def raised(array, own_key, source, target, blocks, factor):
    def block_of(dim):
        return (jnp.arange(array.shape[dim]) // (array.shape[dim] // blocks)).reshape((-1,) + (1,) * (array.ndim - 1 - dim))

    first = jax.random.permutation(own_key, blocks)[block_of(target)]
    far = (block_of(target) + blocks // 2) % blocks
    return jnp.where((block_of(source) == first) | (block_of(source) == far), factor * array, array)


def level_of(stream_key, dims, split, smallest, high):
    loudness, own = 1.0, jax.random.fold_in(stream_key, 6)
    for dim, shards_of in split:
        heights = jnp.exp(jax.random.uniform(jax.random.fold_in(own, dim), (shards_of,), jnp.float32, smallest / len(split), high / len(split)))
        loudness = loudness * jnp.repeat(heights, dims[dim] // shards_of).reshape([-1 if axis == dim else 1 for axis in range(len(dims))])
    return loudness


def scatter_about(own_key, shape, width, most, shards=(), kind=jnp.bfloat16):
    entries = width * jax.random.normal(own_key, shape, jnp.float32)
    if shards:
        entries = entries * level_of(own_key, shape, shards, -0.22, 0.18)
    return jnp.clip(entries, -most, most).astype(kind)


def bell_draw_with(own_key, dims, width, reach, split, heavy, held_as=jnp.bfloat16):
    values = width * jax.random.normal(own_key, dims, jnp.float32)
    if split:
        values = values * level_of(own_key, dims, split, -0.22, 0.18)
    return jnp.clip(raised(values, jax.random.fold_in(own_key, 3), *heavy), -reach, reach).astype(held_as)


def setup_inputs(seed: int = 0) -> dict:
    splits = jax.random.split(jax.random.key(seed), 7)
    return {
        "hidden_in": bell_draw_with(splits[0], (CLIPS, TOKENS, D), 0.5, 4.0, ((0, 16), (1, 16)), (1, 2, 16, 2.0)),
        "spatial_qkv": scatter_about(splits[1], (CLIPS, TOKENS, QKV), 1.0, 6.0, ((0, 16), (1, 16))),
        "temporal_grad": scatter_about(splits[2], (CLIPS, TOKENS, D), 1.0, 6.0, ((0, 16), (1, 16))),
        "pair_grad": scatter_about(splits[3], (CLIPS, TOKENS, D), 0.5, 4.0, ((0, 16), (1, 16))),
        "spatial_proj": scatter_about(splits[4], (D, D), D ** -0.5, 0.1875, ((0, 16),)),
        "temporal_weight": scatter_about(splits[5], (D, QKV), D ** -0.5, 0.1875, ((0, 16),)),
    }


def softmax_parts(packed, layout):
    leading = packed.shape[0]
    second = packed.shape[1]
    head_dim = packed.shape[2] // (3 * HEADS)
    pieces = packed.astype(jnp.float32).reshape(leading, second, 3, HEADS, head_dim)
    queries = pieces[:, :, 0]
    key_rows = pieces[:, :, 1]
    values = pieces[:, :, 2]
    key_layout = layout.replace("i", "j")
    logits = jnp.einsum(layout + "," + key_layout + "->bhij", queries, key_rows) * head_dim ** -0.5
    exponents = jnp.exp(logits)
    attn_probs = exponents / jnp.sum(exponents, axis=-1, keepdims=True)
    rounded = attn_probs.astype(jnp.bfloat16)
    return attn_probs, rounded, queries, key_rows, values


def attend(saved, layout):
    attn_probs, rounded, queries, key_rows, values = saved
    key_layout = layout.replace("i", "j")
    attended = jnp.einsum("bhij," + key_layout + "->" + layout, rounded.astype(jnp.float32), values)
    return attended.reshape(attended.shape[0], attended.shape[1], -1).astype(jnp.bfloat16)


def attend_back(saved, out_grad, layout):
    attn_probs, rounded, queries, key_rows, values = saved
    key_layout = layout.replace("i", "j")
    head_dim = queries.shape[3]
    upstream = out_grad.astype(jnp.float32).reshape(out_grad.shape[0], out_grad.shape[1], HEADS, head_dim)
    value_grad = jnp.einsum("bhij," + layout + "->" + key_layout, rounded.astype(jnp.float32), upstream)
    prob_grad = jnp.einsum(layout + "," + key_layout + "->bhij", upstream, values)
    centre = jnp.sum(attn_probs * prob_grad, axis=-1, keepdims=True)
    logit_grad = (attn_probs * (prob_grad - centre) * head_dim ** -0.5).astype(jnp.bfloat16).astype(jnp.float32)
    query_grad = jnp.einsum("bhij," + key_layout + "->" + layout, logit_grad, key_rows)
    key_grad = jnp.einsum("bhij," + layout + "->" + key_layout, logit_grad, queries)
    stacked = jnp.stack([query_grad, key_grad, value_grad], axis=2)
    return stacked.reshape(stacked.shape[0], stacked.shape[1], -1).astype(jnp.bfloat16)


def block_sum(running_sum, pair_data):
    left_rows, right_rows = pair_data
    partial_sum = jnp.dot(left_rows.T, right_rows, preferred_element_type=jnp.float32).astype(jnp.bfloat16)
    return running_sum + partial_sum.astype(jnp.float32), None


def reference(hidden_in, spatial_qkv, temporal_grad, pair_grad, spatial_proj, temporal_weight):
    def one_clip(running, clip_data):
        hidden_one, spatial_one, temporal_one, pair_one = clip_data
        spatial_saved = softmax_parts(spatial_one.reshape(F, P_SIZE, QKV), "bihd")
        spatial_out = attend(spatial_saved, "bihd").reshape(TOKENS, D)
        branch_out = jnp.dot(spatial_out, spatial_proj, preferred_element_type=jnp.float32)
        block_out = (hidden_one.astype(jnp.float32) + branch_out).astype(jnp.bfloat16)
        packed_t = jnp.dot(block_out, temporal_weight, preferred_element_type=jnp.float32).astype(jnp.bfloat16).reshape(F, P_SIZE, QKV)
        temporal_saved = softmax_parts(packed_t, "ibhd")
        packed_grad = attend_back(temporal_saved, temporal_one.reshape(F, P_SIZE, D), "ibhd").reshape(TOKENS, QKV)
        through = jnp.dot(packed_grad, temporal_weight.T, preferred_element_type=jnp.float32).astype(jnp.bfloat16)
        hidden_grad = (pair_one.astype(jnp.float32) + through.astype(jnp.float32)).astype(jnp.bfloat16)
        spatial_back = jnp.dot(hidden_grad, spatial_proj.T, preferred_element_type=jnp.float32).astype(jnp.bfloat16).reshape(F, P_SIZE, D)
        spatial_grad = attend_back(spatial_saved, spatial_back, "bihd").reshape(TOKENS, QKV)
        input_blocks = block_out.reshape(F, N_SEQ, PATCH_DEV, D).transpose(1, 0, 2, 3).reshape(N_SEQ, F * PATCH_DEV, D)
        grad_blocks = packed_grad.reshape(F, N_SEQ, PATCH_DEV, QKV).transpose(1, 0, 2, 3).reshape(N_SEQ, F * PATCH_DEV, QKV)
        temporal_total = lax.scan(block_sum, jnp.zeros((D, QKV), jnp.float32), (input_blocks, grad_blocks))[0]
        spatial_total = lax.scan(block_sum, jnp.zeros((D, D), jnp.float32), (spatial_out.reshape(N_SEQ, FR_DEV * P_SIZE, D), hidden_grad.reshape(N_SEQ, FR_DEV * P_SIZE, D)))[0]
        return (running[0] + spatial_total, running[1] + temporal_total), (spatial_grad, hidden_grad)

    start_sums = (jnp.zeros((D, D), jnp.float32), jnp.zeros((D, QKV), jnp.float32))
    sums, stacked = lax.scan(one_clip, start_sums, (hidden_in, spatial_qkv, temporal_grad, pair_grad))
    norm_factor = (CLIPS * TOKENS) ** -0.5
    return (stacked[0], stacked[1], (sums[0] * norm_factor).astype(jnp.bfloat16), (sums[1] * norm_factor).astype(jnp.bfloat16))
```

```python
import functools
import math

import jax
import jax.numpy as jnp
from jax import lax
from jax.experimental import pallas as pl
from jax.experimental.pallas import tpu as pltpu
from jax.sharding import Mesh, PartitionSpec as P

HEADS = 16
HEAD_DIM = 72
P_SIZE = 256
D = HEADS * HEAD_DIM
QKV = 3 * D
F = 16
SCALE = HEAD_DIM ** -0.5
EXP2_SCALE = SCALE * math.log2(math.e)
ROWS = 72
Z = 8
HALF = 1792
OFF = QKV - HALF
BF = jnp.bfloat16
F32 = jnp.float32


def head_window(head):
    low = head * HEAD_DIM
    start = low // 128 * 128
    stop = -(-(low + HEAD_DIM) // 128) * 128
    return low, start, stop


def lanes_of(head, rows):
    low, start, stop = head_window(head)
    lane = lax.broadcasted_iota(jnp.int32, (rows, stop - start), 1) + start
    return (lane >= low) & (lane < low + HEAD_DIM)


def nt(a, b):
    return lax.dot_general(a, b, (((1,), (1,)), ((), ())), preferred_element_type=F32)


def nn(a, b):
    return lax.dot_general(a, b, (((1,), (0,)), ((), ())), preferred_element_type=F32)


def tn(a, b):
    return lax.dot_general(a, b, (((0,), (0,)), ((), ())), preferred_element_type=F32)


def add_window(tiles, start, stop, value):
    for index in range(start // 128, stop // 128):
        part = value[:, index * 128 - start:(index + 1) * 128 - start]
        tiles[index] = part if index not in tiles else tiles[index] + part


def flush(tiles, ref, base, upto):
    for index in sorted(tiles):
        if (index + 1) * 128 <= upto:
            ref[:, base + index * 128:base + (index + 1) * 128] = tiles.pop(index).astype(BF)


def forward_kernel(qkv_ref, out_ref):
    rows = qkv_ref.shape[0]
    tiles = {}
    for head in range(HEADS):
        low, start, stop = head_window(head)
        keep = lanes_of(head, rows)
        queries = jnp.where(keep, qkv_ref[:, start:stop], 0)
        keys = qkv_ref[:, D + start:D + stop]
        values = jnp.where(keep, qkv_ref[:, 2 * D + start:2 * D + stop], 0)
        powers = jnp.exp2(nt(queries, keys) * EXP2_SCALE)
        probs = powers / jnp.sum(powers, axis=1, keepdims=True)
        add_window(tiles, start, stop, nn(probs.astype(BF), values))
        flush(tiles, out_ref, 0, low + HEAD_DIM)


def backward_kernel(masked, qkv_ref, grad_ref, out_ref):
    rows = qkv_ref.shape[0]
    if masked:
        one = lax.broadcasted_iota(jnp.int32, (rows, rows), 0)
        two = lax.broadcasted_iota(jnp.int32, (rows, rows), 1)
        same = ((one ^ two) & (rows // F - 1)) == 0
    tiles_q, tiles_k, tiles_v = {}, {}, {}
    for head in range(HEADS):
        low, start, stop = head_window(head)
        keep = lanes_of(head, rows)
        queries = jnp.where(keep, qkv_ref[:, start:stop], 0)
        keys = jnp.where(keep, qkv_ref[:, D + start:D + stop], 0)
        values = qkv_ref[:, 2 * D + start:2 * D + stop]
        upstream = jnp.where(keep, grad_ref[:, start:stop], 0)
        powers = jnp.exp2(nt(keys, queries) * EXP2_SCALE)
        if masked:
            powers = jnp.where(same, powers, 0.0)
        probs = powers * (1.0 / jnp.sum(powers, axis=0, keepdims=True))
        prob_grad = nt(values, upstream)
        if masked:
            prob_grad = jnp.where(same, prob_grad, 0.0)
        weighted = probs * prob_grad
        centre = jnp.sum(weighted, axis=0, keepdims=True)
        logit_grad = ((weighted - probs * centre) * SCALE).astype(BF)
        add_window(tiles_v, start, stop, nn(probs.astype(BF), upstream))
        add_window(tiles_k, start, stop, nn(logit_grad, queries))
        add_window(tiles_q, start, stop, tn(logit_grad, keys))
        flush(tiles_q, out_ref, 0, low + HEAD_DIM)
        flush(tiles_k, out_ref, D, low + HEAD_DIM)
        flush(tiles_v, out_ref, 2 * D, low + HEAD_DIM)


def attention_forward(qkv):
    return pl.pallas_call(
        forward_kernel,
        out_shape=jax.ShapeDtypeStruct((qkv.shape[0], D), BF),
        compiler_params=pltpu.CompilerParams(vmem_limit_bytes=32 * 1024 * 1024),
        cost_estimate=pl.CostEstimate(flops=2 * 2 * HEADS * 256 ** 3, bytes_accessed=4 << 20, transcendentals=1 << 20),
        name="attend",
    )(qkv)


def attention_backward(qkv, grad, masked):
    return pl.pallas_call(
        functools.partial(backward_kernel, masked),
        out_shape=jax.ShapeDtypeStruct(qkv.shape, BF),
        compiler_params=pltpu.CompilerParams(vmem_limit_bytes=32 * 1024 * 1024),
        cost_estimate=pl.CostEstimate(flops=5 * 2 * HEADS * 256 ** 3, bytes_accessed=6 << 20, transcendentals=1 << 20),
        name="attend_back",
    )(qkv, grad)


def turn(size, by):
    return [(index, (index + by) % size) for index in range(size)]


def along_z(array, by):
    return lax.ppermute(array, "z", turn(Z, by))


def along_x(array, by):
    return lax.ppermute(array, "x", turn(4, by))


def across_cores(array):
    return lax.ppermute(array, "c", [(0, 1), (1, 0)])


def gather_z(unit, far_forward):
    ahead, behind = [unit], [unit]
    for step in range(1, 4):
        ahead.append(along_z(ahead[-1], -1))
        behind.append(along_z(behind[-1], 1))
    far = along_z(ahead[-1], -1) if far_forward else along_z(behind[-1], 1)
    return ahead + [far] + behind[:0:-1]


def scatter_sum_z(units):
    def plus(one, two):
        return (one.astype(F32) + two.astype(F32)).astype(BF)

    ahead = along_z(units[4], 1)
    behind = along_z(units[5], -1)
    for step in (3, 2, 1):
        ahead = along_z(plus(ahead, units[step]), 1)
    for step in (6, 7):
        behind = along_z(plus(behind, units[step]), -1)
    return units[0].astype(F32) + ahead.astype(F32) + behind.astype(F32)


def dot(a, b):
    return jnp.dot(a, b, preferred_element_type=F32)


def per_device(hidden_in, spatial_qkv, temporal_grad, pair_grad, spatial_proj, temporal_weight):
    z, y_lo, x, core = (lax.axis_index(name) for name in ("z", "yl", "x", "c"))
    x_odd = x % 2
    home = core == y_lo
    hidden_in = hidden_in.reshape(P_SIZE, D)
    spatial_qkv = spatial_qkv.reshape(P_SIZE, QKV)
    temporal_grad = temporal_grad.reshape(P_SIZE, D)
    pair_grad = pair_grad.reshape(P_SIZE, D)

    place = lax.broadcasted_iota(jnp.int32, (D, D), 1)
    whole = lax.broadcasted_iota(jnp.int32, (D, D), 0)
    side = place // (D // 2)
    spot = place % (D // 2)
    source = ROWS * (2 * ((z + spot // ROWS) % Z) + (core + side) % 2) + spot % ROWS
    order = (whole == source).astype(BF)

    def to_home(array):
        moved = lax.ppermute(array, ("yl", "c"), [(0, 2), (3, 1)])
        return jnp.where(home, array, moved)

    weight_half = lax.dynamic_slice(temporal_weight, (0, x_odd * OFF), (ROWS, HALF))
    proj_units = gather_z(to_home(spatial_proj), True)
    weight_units = gather_z(to_home(weight_half), False)
    proj_mine = jnp.concatenate(proj_units, axis=0)
    proj = jnp.concatenate([proj_mine, across_cores(proj_mine)], axis=0)
    other_units = [along_x(unit, 1) for unit in weight_units[:4]] + [along_x(unit, -1) for unit in weight_units[4:]]
    mine = jnp.concatenate(weight_units, axis=0)
    other = jnp.concatenate(other_units, axis=0)
    mine = jnp.concatenate([mine, across_cores(mine)], axis=0)
    other = jnp.concatenate([other, across_cores(other)], axis=0)

    spatial_out = attention_forward(spatial_qkv)
    spatial_rel = dot(spatial_out, order).astype(BF)
    block_out = (hidden_in.astype(F32) + dot(spatial_rel, proj)).astype(BF)

    def to_patches(array):
        return lax.all_to_all(
            array.reshape(1, P_SIZE, D), ("z", "yl"), split_axis=1, concat_axis=0, tiled=True
        ).reshape(P_SIZE, D)

    grad_t = to_patches(temporal_grad)
    block_t = to_patches(block_out)
    block_rel = dot(block_t, order).astype(BF)

    qkv_mine = dot(block_rel, mine).astype(BF)
    qkv_other = dot(block_rel, other).astype(BF)
    first = jnp.where(x_odd == 0, qkv_mine, qkv_other)
    second = jnp.where(x_odd == 0, qkv_other, qkv_mine)
    qkv_t = jnp.concatenate([first, second[:, HALF - OFF:]], axis=1)
    packed_grad = attention_backward(qkv_t, grad_t, True)
    low_part = packed_grad[:, :HALF]
    high_part = packed_grad[:, OFF:]
    grad_mine = jnp.where(x_odd == 0, low_part, high_part)
    grad_other = jnp.where(x_odd == 0, high_part, low_part)
    column = lax.broadcasted_iota(jnp.int32, (1, HALF), 1)
    once = jnp.where((x_odd == 0) & (column < HALF - OFF), 0, 1).astype(BF)
    drop = jnp.where((x_odd == 0) | (column >= HALF - OFF), 1, 0).astype(BF)
    through_rel = (nt(grad_mine * drop, mine) + nt(grad_other * once, other)).astype(BF)
    through = nt(through_rel, order).astype(BF)
    returned = lax.all_to_all(
        through.reshape(F, P_SIZE // F, D), ("z", "yl"), split_axis=0, concat_axis=1, tiled=True
    ).reshape(P_SIZE, D)
    hidden_grad = (pair_grad.astype(F32) + returned.astype(F32)).astype(BF)

    half = D // 2
    block_pair = jnp.concatenate([block_rel[:, :half], across_cores(block_rel[:, half:])], axis=0)
    packed_pair = jnp.concatenate([packed_grad, across_cores(packed_grad)], axis=0)
    pair_low, pair_high = packed_pair[:, :HALF], packed_pair[:, OFF:]
    stay = tn(block_pair, jnp.where(x_odd == 0, pair_low, pair_high)).astype(BF)
    leave = tn(block_pair, jnp.where(x_odd == 0, pair_high, pair_low)).astype(BF)
    came = jnp.concatenate([along_x(leave[:half // 2], 1), along_x(leave[half // 2:], -1)], axis=0)
    stay = (stay.astype(F32) + came.astype(F32)).astype(BF).reshape(Z, ROWS, HALF)
    weight_sum = scatter_sum_z([stay[index] for index in range(Z)]).astype(BF)

    spatial_pair = jnp.concatenate([spatial_rel[:, :half], across_cores(spatial_rel[:, half:])], axis=0)
    hidden_pair = jnp.concatenate([hidden_grad, across_cores(hidden_grad)], axis=0)
    proj_part = tn(spatial_pair, hidden_pair).astype(BF).reshape(Z, ROWS, D)
    proj_sum = scatter_sum_z([proj_part[index] for index in range(Z)]).astype(BF)

    spatial_back = nt(nt(hidden_grad, proj).astype(BF), order).astype(BF)
    spatial_grad = attention_backward(spatial_qkv, spatial_back, False)

    weight_in = lax.ppermute(weight_sum, ("yl", "c"), [(2, 0), (1, 3)])
    proj_near = across_cores(proj_sum)
    proj_far = lax.ppermute(proj_sum, ("yl", "c"), [(1, 2), (2, 1)])
    weight_two = weight_sum.astype(F32) + weight_in.astype(F32)
    proj_two = proj_near.astype(F32) + proj_far.astype(F32)
    total = jnp.where(home, weight_two, jnp.pad(proj_two, ((0, 0), (0, HALF - D))))
    sent = total.astype(BF)
    total = (sent.astype(F32) + lax.ppermute(sent, "yh", [(0, 1), (1, 0)]).astype(F32)).astype(BF)
    total = (total.astype(F32) + along_x(total, 2).astype(F32)).astype(BF)
    beside = lax.ppermute(total, "x", [(0, 1), (1, 0), (2, 3), (3, 2)])
    mate_total = across_cores(total)
    mate_beside = across_cores(beside)
    proj_a = jnp.where(home, mate_total, total)[:, :D].astype(F32)
    proj_b = jnp.where(home, mate_beside, beside)[:, :D].astype(F32)
    weight_a = jnp.where(home, total, mate_total)
    weight_b = jnp.where(home, beside, mate_beside)
    low = jnp.where(x_odd == 0, weight_a, weight_b)
    high = jnp.where(x_odd == 0, weight_b, weight_a)
    weight_all = jnp.concatenate([low, high[:, HALF - OFF:]], axis=1)
    norm = (16 * 4096) ** -0.5
    return (
        spatial_grad.reshape(1, P_SIZE, QKV),
        hidden_grad.reshape(1, P_SIZE, D),
        ((proj_a + proj_b) * norm).astype(BF),
        (weight_all.astype(F32) * norm).astype(BF),
    )


def solution(mesh):
    fine = Mesh(mesh.devices.reshape(8, 2, 2, 4, 2), ("z", "yl", "yh", "x", "c"))
    tokens = P(("yh", "x", "c"), ("z", "yl"), None)
    rows = P(("z", "yl"), None)
    return jax.shard_map(
        per_device,
        mesh=fine,
        in_specs=(tokens, tokens, tokens, tokens, rows, rows),
        out_specs=(tokens, tokens, rows, rows),
        check_vma=False,
    )
```

```python
import functools
import math

import jax
import jax.numpy as jnp
from jax import lax
from jax.experimental import pallas as pl
from jax.experimental.pallas import tpu as pltpu
from jax.sharding import Mesh, PartitionSpec as P

HEADS = 16
HEAD_DIM = 72
P_SIZE = 256
D = HEADS * HEAD_DIM
QKV = 3 * D
F = 16
SCALE = HEAD_DIM ** -0.5
EXP2_SCALE = SCALE * math.log2(math.e)
ROWS = 72
UNIT = 2 * ROWS
Z = 8
WIDE = 896
PW = 640
NORM = (16 * 4096) ** -0.5
BF = jnp.bfloat16
F32 = jnp.float32


def wide_start(index):
    return 128 * (7 * index - (index >= 2))


def head_window(head):
    low = head * HEAD_DIM
    start = low // 128 * 128
    stop = -(-(low + HEAD_DIM) // 128) * 128
    return low, start, stop


def lanes_of(head, rows):
    low, start, stop = head_window(head)
    lane = lax.broadcasted_iota(jnp.int32, (rows, stop - start), 1) + start
    return (lane >= low) & (lane < low + HEAD_DIM)


def nt(a, b):
    return lax.dot_general(a, b, (((1,), (1,)), ((), ())), preferred_element_type=F32)


def nn(a, b):
    return lax.dot_general(a, b, (((1,), (0,)), ((), ())), preferred_element_type=F32)


def tn(a, b):
    return lax.dot_general(a, b, (((0,), (0,)), ((), ())), preferred_element_type=F32)


def add_window(tiles, start, stop, value):
    for index in range(start // 128, stop // 128):
        part = value[:, index * 128 - start:(index + 1) * 128 - start]
        tiles[index] = part if index not in tiles else tiles[index] + part


def flush(tiles, ref, base, upto):
    for index in sorted(tiles):
        if (index + 1) * 128 <= upto:
            ref[:, base + index * 128:base + (index + 1) * 128] = tiles.pop(index).astype(BF)


def forward_kernel(qkv_ref, out_ref):
    rows = qkv_ref.shape[0]
    tiles = {}
    for head in range(HEADS):
        low, start, stop = head_window(head)
        keep = lanes_of(head, rows)
        queries = jnp.where(keep, qkv_ref[:, start:stop], 0)
        keys = qkv_ref[:, D + start:D + stop]
        values = jnp.where(keep, qkv_ref[:, 2 * D + start:2 * D + stop], 0)
        powers = jnp.exp2(nt(queries, keys) * EXP2_SCALE)
        probs = powers / jnp.sum(powers, axis=1, keepdims=True)
        add_window(tiles, start, stop, nn(probs.astype(BF), values))
        flush(tiles, out_ref, 0, low + HEAD_DIM)


def backward(masked, qkv_ref, grad_ref, out_ref):
    rows = qkv_ref.shape[0]
    if masked:
        one = lax.broadcasted_iota(jnp.int32, (rows, rows), 0)
        two = lax.broadcasted_iota(jnp.int32, (rows, rows), 1)
        same = ((one ^ two) & (rows // F - 1)) == 0
    tiles_q, tiles_k, tiles_v = {}, {}, {}
    for head in range(HEADS):
        low, start, stop = head_window(head)
        keep = lanes_of(head, rows)
        queries = jnp.where(keep, qkv_ref[:, start:stop], 0)
        keys = jnp.where(keep, qkv_ref[:, D + start:D + stop], 0)
        values = qkv_ref[:, 2 * D + start:2 * D + stop]
        upstream = jnp.where(keep, grad_ref[:, start:stop], 0)
        powers = jnp.exp2(nt(keys, queries) * EXP2_SCALE)
        if masked:
            powers = jnp.where(same, powers, 0.0)
        probs = powers * (1.0 / jnp.sum(powers, axis=0, keepdims=True))
        prob_grad = nt(values, upstream)
        if masked:
            prob_grad = jnp.where(same, prob_grad, 0.0)
        weighted = probs * prob_grad
        centre = jnp.sum(weighted, axis=0, keepdims=True)
        logit_grad = ((weighted - probs * centre) * SCALE).astype(BF)
        add_window(tiles_v, start, stop, nn(probs.astype(BF), upstream))
        add_window(tiles_k, start, stop, nn(logit_grad, queries))
        add_window(tiles_q, start, stop, tn(logit_grad, keys))
        flush(tiles_q, out_ref, 0, low + HEAD_DIM)
        flush(tiles_k, out_ref, D, low + HEAD_DIM)
        flush(tiles_v, out_ref, 2 * D, low + HEAD_DIM)


VMEM = pl.BlockSpec(memory_space=pltpu.VMEM)
SMEM = pl.BlockSpec(memory_space=pltpu.SMEM)
ANY = pl.BlockSpec(memory_space=pl.ANY)


def shape(*dims):
    return jax.ShapeDtypeStruct(dims, BF)


def call(kernel, name, out_shape, in_specs, out_specs, scratch=(), flops=0, moved=0, limit=32):
    return pl.pallas_call(
        kernel,
        out_shape=out_shape,
        in_specs=in_specs,
        out_specs=out_specs,
        scratch_shapes=scratch,
        compiler_params=pltpu.CompilerParams(vmem_limit_bytes=limit << 20),
        cost_estimate=pl.CostEstimate(flops=flops, bytes_accessed=moved, transcendentals=0),
        name=name,
    )


def columns(ref, start, width):
    return ref[:, pl.ds(pl.multiple_of(start, 128), width)]


def from_second_tile(value, shared):
    lane = lax.broadcasted_iota(jnp.int32, value.shape, 1)
    return jnp.where((lane < 128) & shared, jnp.zeros_like(value), value)


def block_kernel(at_ref, hidden_ref, out_ref, proj_ref, mate_ref, block_ref):
    for index, weight in enumerate((proj_ref, mate_ref)):
        start = pl.multiple_of(at_ref[index], 128)
        total = columns(hidden_ref, start, PW).astype(F32) + nn(out_ref[...], weight[...])
        block_ref[:, pl.ds(start, PW)] = total.astype(BF)


def temporal_kernel(at_ref, block_ref, grad_ref, w0, w1, w2, w3, through_ref, keep_ref, send_ref, held, qkv, packed, sems):
    copies = [pltpu.make_async_copy(w, held.at[index], sems.at[index]) for index, w in enumerate((w0, w1, w2, w3))]
    for copy in copies:
        copy.start()
    for index, copy in enumerate(copies):
        copy.wait()
        start = pl.multiple_of(at_ref[index], 128)
        qkv[:, pl.ds(start, WIDE)] = nn(block_ref[...], held[index]).astype(BF)
    backward(True, qkv, grad_ref, packed)
    through = None
    for index in range(4):
        part = columns(packed, at_ref[index], WIDE)
        (send_ref if index % 2 else keep_ref)[:, index // 2 * WIDE:(index // 2 + 1) * WIDE] = part
        term = nt(from_second_tile(part, at_ref[index] == wide_start(2)), held[index])
        through = term if through is None else through + term
    through_ref[...] = through.astype(BF)


def spatial_kernel(at_ref, qkv_ref, hidden_ref, proj_ref, mate_ref, out_ref, back):
    total = None
    for index, weight in enumerate((proj_ref, mate_ref)):
        start = at_ref[index]
        term = nt(from_second_tile(columns(hidden_ref, start, PW), start > 0), weight[...])
        total = term if total is None else total + term
    back[...] = total.astype(BF)
    backward(False, qkv_ref, back, out_ref)


def product_kernel(where, z_ref, left0, left1, right0, right1, *rest):
    outs, lefts, rights, total = rest[:-3], rest[-3], rest[-2], rest[-1]
    lefts[:P_SIZE] = left0[...]
    lefts[P_SIZE:] = left1[...]
    rights[:P_SIZE] = right0[...]
    rights[P_SIZE:] = right1[...]
    total[...] = tn(lefts[...], rights[...]).astype(BF)
    for out, units in zip(outs, where):
        for place, unit in enumerate(units):
            row = pl.multiple_of(lax.rem(z_ref[0] + unit, Z) * UNIT, 16)
            out[place * UNIT:(place + 1) * UNIT, :] = total[pl.ds(row, UNIT), :]


def product(name, z, left0, left1, right0, right1, where):
    width = right0.shape[1]
    return call(
        functools.partial(product_kernel, where), name,
        [shape(UNIT * len(units), width) for units in where],
        [SMEM] + [VMEM] * 4, [VMEM] * len(where),
        [pltpu.VMEM((2 * P_SIZE, D), BF), pltpu.VMEM((2 * P_SIZE, width), BF), pltpu.VMEM((D, width), BF)],
        flops=4 * P_SIZE * D * width, moved=6 << 20,
    )(z, left0, left1, right0, right1)


def place_kernel(where, z_ref, *rest):
    parts, out, sems = rest[:len(where)], rest[-2], rest[-1]
    copies = []
    for part, units in zip(parts, where):
        for place, unit in enumerate(units):
            row = pl.multiple_of(lax.rem(z_ref[0] + unit, Z) * UNIT, 16)
            copies.append(pltpu.make_async_copy(
                part.at[pl.ds(place * UNIT, UNIT)], out.at[pl.ds(row, UNIT)], sems.at[len(copies)]))
    for copy in copies:
        copy.start()
    for copy in copies:
        copy.wait()


def placed(name, z, parts, where):
    width = parts[0].shape[1]
    return call(
        functools.partial(place_kernel, where), name, shape(D, width),
        [SMEM] + [ANY] * len(parts), ANY, [pltpu.SemaphoreType.DMA((Z,))], moved=4 << 20,
    )(z, *parts)


def finish_kernel(at_ref, pat_ref, mine_ref, mate_ref, mine_p, mate_p, weight_ref, proj_ref):
    for index in range(4):
        source = mate_ref if index % 2 else mine_ref
        part = source[:, index // 2 * WIDE:(index // 2 + 1) * WIDE]
        start = pl.multiple_of(at_ref[index], 128)
        weight_ref[:, pl.ds(start, WIDE)] = (part.astype(F32) * NORM).astype(BF)
    for index, source in enumerate((mine_p, mate_p)):
        start = pl.multiple_of(pat_ref[index], 128)
        proj_ref[:, pl.ds(start, PW)] = (source[...].astype(F32) * NORM).astype(BF)


def along_z(array, by):
    return lax.ppermute(array, "z", [(index, (index + by) % Z) for index in range(Z)])


def along_plane(array, by_x, by_y):
    pairs = []
    for lo in range(2):
        for hi in range(2):
            for x in range(4):
                y = (2 * hi + lo + by_y) % 4
                pairs.append(((lo * 2 + hi) * 4 + x, (y % 2 * 2 + y // 2) * 4 + (x + by_x) % 4))
    return lax.ppermute(array, ("yl", "yh", "x"), pairs)


def across_cores(array):
    return lax.ppermute(array, "c", [(0, 1), (1, 0)])


def plus(one, *more):
    total = one.astype(F32)
    for value in more:
        total = total + value.astype(F32)
    return total.astype(BF)


SHARE = ((0, 1), (7, 2), (6, 3), (5, 4))
STEPS = ((1, 0), (-1, 0), (0, 1), (0, -1))


def per_device(hidden_in, spatial_qkv, temporal_grad, pair_grad, spatial_proj, temporal_weight):
    z, y_lo, x, core = (lax.axis_index(name) for name in ("z", "yl", "x", "c"))
    odd = (x + y_lo) % 2
    z_at = z.reshape(1)
    hidden_in = hidden_in.reshape(P_SIZE, D)
    spatial_qkv = spatial_qkv.reshape(P_SIZE, QKV)
    pair_grad = pair_grad.reshape(P_SIZE, D)

    ranges = [wide_start(2 * parity + side) for parity in (odd, 1 - odd) for side in (core, 1 - core)]
    wide_at = jnp.stack(ranges)
    proj_at = jnp.stack([512 * core, 512 * (1 - core)])

    def both_rows(mine, theirs):
        came = lax.ppermute(theirs, "yl", [(0, 1), (1, 0)])
        return jnp.where(y_lo == 0, jnp.concatenate([mine, came]), jnp.concatenate([came, mine]))

    proj_part = lax.dynamic_slice(spatial_proj, (0, proj_at[0]), (ROWS, PW))
    unit = both_rows(
        jnp.concatenate([proj_part, lax.dynamic_slice(temporal_weight, (0, ranges[0]), (ROWS, WIDE))], axis=1),
        jnp.concatenate([proj_part, lax.dynamic_slice(temporal_weight, (0, ranges[2]), (ROWS, WIDE))], axis=1),
    )
    proj = lax.all_gather(unit[:, :PW], "z", axis=0, tiled=True)
    proj_mate = across_cores(proj)
    ahead, behind = [unit[:, PW:]], [unit[:, PW:]]
    for step in range(1, 4):
        ahead.append(along_z(ahead[-1], -1))
        behind.append(along_z(behind[-1], 1))
    units = ahead + [along_z(ahead[-1], -1)] + behind[:0:-1]
    came = [
        along_plane(jnp.concatenate([units[index] for index in share]), *step) for share, step in zip(SHARE, STEPS)
    ]
    weight_mine = placed("place_mine", z_at, units, [(index,) for index in range(Z)])
    weight_other = placed("place_other", z_at, came, SHARE)
    weights = (weight_mine, across_cores(weight_mine), weight_other, across_cores(weight_other))

    def exchange(array):
        return lax.all_to_all(
            array.reshape(16, F, D), ("z", "yl"), split_axis=0, concat_axis=0, tiled=True
        ).reshape(P_SIZE, D)

    grad_t = exchange(temporal_grad)
    spatial_out = call(
        forward_kernel, "attend", shape(P_SIZE, D), [VMEM], VMEM, flops=4 * HEADS * 256 ** 3, moved=4 << 20
    )(spatial_qkv)
    spatial_mate = across_cores(spatial_out)
    block_out = call(
        block_kernel, "block", shape(P_SIZE, D), [SMEM] + [VMEM] * 4, VMEM, flops=2 * P_SIZE * D * D, moved=5 << 20
    )(proj_at, hidden_in, spatial_out, proj, proj_mate)
    block_t = exchange(block_out)
    block_mate = across_cores(block_t)

    through, keep, send = call(
        temporal_kernel, "temporal",
        [shape(P_SIZE, D), shape(P_SIZE, 2 * WIDE), shape(P_SIZE, 2 * WIDE)],
        [SMEM, VMEM, VMEM] + [ANY] * 4, [VMEM] * 3,
        [
            pltpu.VMEM((4, D, WIDE), BF), pltpu.VMEM((P_SIZE, QKV), BF), pltpu.VMEM((P_SIZE, QKV), BF),
            pltpu.SemaphoreType.DMA((4,)),
        ],
        flops=4 * P_SIZE * D * QKV + 10 * HEADS * 256 ** 3, moved=16 << 20, limit=40,
    )(wide_at, block_t, grad_t, *weights)
    returned = exchange(through)

    packed_mate = across_cores(send)
    leave = product("leave", z_at, block_t, block_mate, keep[:, WIDE:], packed_mate[:, WIDE:], SHARE)
    came = [along_plane(part, *step) for part, step in zip(leave[::-1], STEPS[::-1])][::-1]
    stay = product(
        "stay", z_at, block_t, block_mate, keep[:, :WIDE], packed_mate[:, :WIDE], [(index,) for index in range(Z)]
    )
    arrived = {}
    for part, share in zip(came, SHARE):
        for place, index in enumerate(share):
            arrived[index] = part[place * UNIT:(place + 1) * UNIT]
    ahead = along_z(plus(stay[4], arrived[4]), 1)
    behind = along_z(plus(stay[5], arrived[5]), -1)
    for up, down in ((3, 6), (2, 7)):
        ahead = along_z(plus(stay[up], arrived[up], ahead), 1)
        behind = along_z(plus(stay[down], arrived[down], behind), -1)
    ahead = along_z(plus(stay[1], arrived[1], ahead), 1)
    weight_sum = plus(stay[0], arrived[0], ahead, behind)

    hidden_grad = plus(pair_grad, returned)
    hidden_mine = lax.dynamic_slice(hidden_grad, (0, proj_at[0]), (P_SIZE, PW))
    hidden_mate = across_cores(lax.dynamic_slice(hidden_grad, (0, proj_at[1]), (P_SIZE, PW)))
    (proj_part,) = product(
        "proj_part", jnp.zeros_like(z_at), spatial_out, spatial_mate, hidden_mine, hidden_mate, [tuple(range(Z))]
    )
    proj_sum = lax.psum_scatter(proj_part, "z", scatter_dimension=0, tiled=True)
    spatial_grad = call(
        spatial_kernel, "spatial", shape(P_SIZE, QKV), [SMEM] + [VMEM] * 4, VMEM, [pltpu.VMEM((P_SIZE, D), BF)],
        flops=2 * P_SIZE * D * D + 10 * HEADS * 256 ** 3, moved=8 << 20,
    )(proj_at, spatial_qkv, hidden_grad, proj, proj_mate)

    both = jnp.concatenate([weight_sum, proj_sum], axis=1)
    total = lax.dynamic_slice(both, (ROWS * y_lo, 0), (ROWS, WIDE + PW))
    total = plus(total, along_plane(lax.dynamic_slice(both, (ROWS * (1 - y_lo), 0), (ROWS, WIDE + PW)), 1, 1))
    total = plus(total, along_plane(total, 2, 0))
    total = plus(total, along_plane(total, 0, 2))
    beside = lax.ppermute(total, "x", [(0, 1), (1, 0), (2, 3), (3, 2)])
    weight_sums = jnp.concatenate([total[:, :WIDE], beside[:, :WIDE]], axis=1)
    proj_sums = plus(total[:, WIDE:], beside[:, WIDE:])
    weight_grad, proj_grad = call(
        finish_kernel, "finish", [shape(ROWS, QKV), shape(ROWS, D)], [SMEM] * 2 + [VMEM] * 4, [VMEM] * 2, moved=2 << 20,
    )(wide_at, proj_at, weight_sums, across_cores(weight_sums), proj_sums, across_cores(proj_sums))
    return (
        spatial_grad.reshape(1, P_SIZE, QKV),
        hidden_grad.reshape(1, P_SIZE, D),
        proj_grad,
        weight_grad,
    )


def solution(mesh):
    fine = Mesh(mesh.devices.reshape(8, 2, 2, 4, 2), ("z", "yl", "yh", "x", "c"))
    tokens = P(("yh", "x", "c"), ("z", "yl"), None)
    rows = P(("z", "yl"), None)
    return jax.shard_map(
        per_device,
        mesh=fine,
        in_specs=(tokens, tokens, tokens, tokens, rows, rows),
        out_specs=(tokens, tokens, rows, rows),
        check_vma=False,
    )
```

```python
import functools
import math

import jax
import jax.numpy as jnp
from jax import lax
from jax.experimental import pallas as pl
from jax.experimental.pallas import tpu as pltpu
from jax.sharding import Mesh, PartitionSpec as P

HEADS = 16
HEAD_DIM = 72
P_SIZE = 256
D = HEADS * HEAD_DIM
QKV = 3 * D
F = 16
SCALE = HEAD_DIM ** -0.5
EXP2_SCALE = SCALE * math.log2(math.e)
ROWS = 72
UNIT = 2 * ROWS
Z = 8
WIDE = 896
PW = 640
NORM = (16 * 4096) ** -0.5
BF = jnp.bfloat16
F32 = jnp.float32


def wide_start(index):
    return 128 * (7 * index - (index >= 2))


def head_window(head):
    low = head * HEAD_DIM
    start = low // 128 * 128
    stop = -(-(low + HEAD_DIM) // 128) * 128
    return low, start, stop


def lanes_of(head, rows):
    low, start, stop = head_window(head)
    lane = lax.broadcasted_iota(jnp.int32, (rows, stop - start), 1) + start
    return (lane >= low) & (lane < low + HEAD_DIM)


def nt(a, b):
    return lax.dot_general(a, b, (((1,), (1,)), ((), ())), preferred_element_type=F32)


def nn(a, b):
    return lax.dot_general(a, b, (((1,), (0,)), ((), ())), preferred_element_type=F32)


def tn(a, b):
    return lax.dot_general(a, b, (((0,), (0,)), ((), ())), preferred_element_type=F32)


def add_window(tiles, start, stop, value):
    for index in range(start // 128, stop // 128):
        part = value[:, index * 128 - start:(index + 1) * 128 - start]
        tiles[index] = part if index not in tiles else tiles[index] + part


def flush(tiles, ref, base, upto):
    for index in sorted(tiles):
        if (index + 1) * 128 <= upto:
            ref[:, base + index * 128:base + (index + 1) * 128] = tiles.pop(index).astype(BF)


def forward_kernel(qkv_ref, out_ref):
    rows = qkv_ref.shape[0]
    tiles = {}
    for head in range(HEADS):
        low, start, stop = head_window(head)
        keep = lanes_of(head, rows)
        queries = jnp.where(keep, qkv_ref[:, start:stop], 0)
        keys = qkv_ref[:, D + start:D + stop]
        values = jnp.where(keep, qkv_ref[:, 2 * D + start:2 * D + stop], 0)
        powers = jnp.exp2(nt(queries, keys) * EXP2_SCALE)
        probs = powers / jnp.sum(powers, axis=1, keepdims=True)
        add_window(tiles, start, stop, nn(probs.astype(BF), values))
        flush(tiles, out_ref, 0, low + HEAD_DIM)


def backward(masked, qkv_ref, grad_ref, out_ref):
    rows = qkv_ref.shape[0]
    if masked:
        one = lax.broadcasted_iota(jnp.int32, (rows, rows), 0)
        two = lax.broadcasted_iota(jnp.int32, (rows, rows), 1)
        same = ((one ^ two) & (rows // F - 1)) == 0
    tiles_q, tiles_k, tiles_v = {}, {}, {}
    for head in range(HEADS):
        low, start, stop = head_window(head)
        keep = lanes_of(head, rows)
        queries = jnp.where(keep, qkv_ref[:, start:stop], 0)
        keys = jnp.where(keep, qkv_ref[:, D + start:D + stop], 0)
        values = qkv_ref[:, 2 * D + start:2 * D + stop]
        upstream = jnp.where(keep, grad_ref[:, start:stop], 0)
        powers = jnp.exp2(nt(keys, queries) * EXP2_SCALE)
        if masked:
            powers = jnp.where(same, powers, 0.0)
        probs = powers * (1.0 / jnp.sum(powers, axis=0, keepdims=True))
        prob_grad = nt(values, upstream)
        if masked:
            prob_grad = jnp.where(same, prob_grad, 0.0)
        weighted = probs * prob_grad
        centre = jnp.sum(weighted, axis=0, keepdims=True)
        logit_grad = ((weighted - probs * centre) * SCALE).astype(BF)
        add_window(tiles_v, start, stop, nn(probs.astype(BF), upstream))
        add_window(tiles_k, start, stop, nn(logit_grad, queries))
        add_window(tiles_q, start, stop, tn(logit_grad, keys))
        flush(tiles_q, out_ref, 0, low + HEAD_DIM)
        flush(tiles_k, out_ref, D, low + HEAD_DIM)
        flush(tiles_v, out_ref, 2 * D, low + HEAD_DIM)


VMEM = pl.BlockSpec(memory_space=pltpu.VMEM)
SMEM = pl.BlockSpec(memory_space=pltpu.SMEM)
ANY = pl.BlockSpec(memory_space=pl.ANY)


def shape(*dims):
    return jax.ShapeDtypeStruct(dims, BF)


def call(kernel, name, out_shape, in_specs, out_specs, scratch=(), flops=0, moved=0, limit=32):
    return pl.pallas_call(
        kernel,
        out_shape=out_shape,
        in_specs=in_specs,
        out_specs=out_specs,
        scratch_shapes=scratch,
        compiler_params=pltpu.CompilerParams(vmem_limit_bytes=limit << 20),
        cost_estimate=pl.CostEstimate(flops=flops, bytes_accessed=moved, transcendentals=0),
        name=name,
    )


def columns(ref, start, width):
    return ref[:, pl.ds(pl.multiple_of(start, 128), width)]


def from_second_tile(value, shared):
    lane = lax.broadcasted_iota(jnp.int32, value.shape, 1)
    return jnp.where((lane < 128) & shared, jnp.zeros_like(value), value)


def block_kernel(at_ref, hidden_ref, out_ref, proj_ref, mate_ref, block_ref):
    for index, weight in enumerate((proj_ref, mate_ref)):
        start = pl.multiple_of(at_ref[index], 128)
        total = columns(hidden_ref, start, PW).astype(F32) + nn(out_ref[...], weight[...])
        block_ref[:, pl.ds(start, PW)] = total.astype(BF)


def temporal_kernel(at_ref, block_ref, grad_ref, w0, w1, w2, w3, through_ref, keep_ref, send_ref, held, qkv, packed, sems):
    copies = [pltpu.make_async_copy(w, held.at[index], sems.at[index]) for index, w in enumerate((w0, w1, w2, w3))]
    for copy in copies:
        copy.start()
    for index, copy in enumerate(copies):
        copy.wait()
        start = pl.multiple_of(at_ref[index], 128)
        qkv[:, pl.ds(start, WIDE)] = nn(block_ref[...], held[index]).astype(BF)
    backward(True, qkv, grad_ref, packed)
    through = None
    for index in range(4):
        part = columns(packed, at_ref[index], WIDE)
        (send_ref if index % 2 else keep_ref)[:, index // 2 * WIDE:(index // 2 + 1) * WIDE] = part
        term = nt(from_second_tile(part, at_ref[index] == wide_start(2)), held[index])
        through = term if through is None else through + term
    through_ref[...] = through.astype(BF)


def spatial_kernel(at_ref, qkv_ref, hidden_ref, proj_ref, mate_ref, out_ref, back):
    total = None
    for index, weight in enumerate((proj_ref, mate_ref)):
        start = at_ref[index]
        term = nt(from_second_tile(columns(hidden_ref, start, PW), start > 0), weight[...])
        total = term if total is None else total + term
    back[...] = total.astype(BF)
    backward(False, qkv_ref, back, out_ref)


def product_kernel(where, column, width, z_ref, left0, left1, right0, right1, *rest):
    outs, lefts, rights, total = rest[:-3], rest[-3], rest[-2], rest[-1]
    lefts[:P_SIZE] = left0[...]
    lefts[P_SIZE:] = left1[...]
    rights[:P_SIZE] = right0[:, column:column + width]
    rights[P_SIZE:] = right1[:, column:column + width]
    total[...] = tn(lefts[...], rights[...]).astype(BF)
    for out, units in zip(outs, where):
        for place, unit in enumerate(units):
            row = pl.multiple_of(lax.rem(z_ref[0] + unit, Z) * UNIT, 16)
            out[place * UNIT:(place + 1) * UNIT, :] = total[pl.ds(row, UNIT), :]


def product(name, z, left0, left1, right0, right1, column, width, where):
    return call(
        functools.partial(product_kernel, where, column, width), name,
        [shape(UNIT * len(units), width) for units in where],
        [SMEM] + [VMEM] * 4, [VMEM] * len(where),
        [pltpu.VMEM((2 * P_SIZE, D), BF), pltpu.VMEM((2 * P_SIZE, width), BF), pltpu.VMEM((D, width), BF)],
        flops=4 * P_SIZE * D * width, moved=6 << 20,
    )(z, left0, left1, right0, right1)


def place_kernel(where, z_ref, *rest):
    parts, out, sems = rest[:len(where)], rest[-2], rest[-1]
    copies = []
    for part, units in zip(parts, where):
        for place, unit in enumerate(units):
            row = pl.multiple_of(lax.rem(z_ref[0] + unit, Z) * UNIT, 16)
            copies.append(pltpu.make_async_copy(
                part.at[pl.ds(place * UNIT, UNIT)], out.at[pl.ds(row, UNIT)], sems.at[len(copies)]))
    for copy in copies:
        copy.start()
    for copy in copies:
        copy.wait()


def placed(name, z, parts, where):
    width = parts[0].shape[1]
    return call(
        functools.partial(place_kernel, where), name, shape(D, width),
        [SMEM] + [ANY] * len(parts), VMEM, [pltpu.SemaphoreType.DMA((Z,))], moved=4 << 20,
    )(z, *parts)


def finish_kernel(at_ref, pat_ref, mine_ref, mate_ref, mine_p, mate_p, weight_ref, proj_ref):
    for index in range(4):
        source = mate_ref if index % 2 else mine_ref
        part = source[:, index // 2 * WIDE:(index // 2 + 1) * WIDE]
        start = pl.multiple_of(at_ref[index], 128)
        weight_ref[:, pl.ds(start, WIDE)] = (part.astype(F32) * NORM).astype(BF)
    for index, source in enumerate((mine_p, mate_p)):
        start = pl.multiple_of(pat_ref[index], 128)
        proj_ref[:, pl.ds(start, PW)] = (source[...].astype(F32) * NORM).astype(BF)


def along_z(array, by):
    return lax.ppermute(array, "z", [(index, (index + by) % Z) for index in range(Z)])


def along_plane(array, by_x, by_y):
    pairs = []
    for lo in range(2):
        for hi in range(2):
            for x in range(4):
                y = (2 * hi + lo + by_y) % 4
                pairs.append(((lo * 2 + hi) * 4 + x, (y % 2 * 2 + y // 2) * 4 + (x + by_x) % 4))
    return lax.ppermute(array, ("yl", "yh", "x"), pairs)


def across_cores(array):
    return lax.ppermute(array, "c", [(0, 1), (1, 0)])


def after(value, *others):
    return lax.optimization_barrier((value, *others))[0]


def plus(one, *more):
    total = one.astype(F32)
    for value in more:
        total = total + value.astype(F32)
    return total.astype(BF)


SHARE = ((0, 1), (7, 2), (6, 3), (5, 4))
STEPS = ((1, 0), (-1, 0), (0, 1), (0, -1))


def per_device(hidden_in, spatial_qkv, temporal_grad, pair_grad, spatial_proj, temporal_weight):
    z, y_lo, x, core = (lax.axis_index(name) for name in ("z", "yl", "x", "c"))
    odd = (x + y_lo) % 2
    z_at = z.reshape(1)
    hidden_in = hidden_in.reshape(P_SIZE, D)
    spatial_qkv = spatial_qkv.reshape(P_SIZE, QKV)
    pair_grad = pair_grad.reshape(P_SIZE, D)

    ranges = [wide_start(2 * parity + side) for parity in (odd, 1 - odd) for side in (core, 1 - core)]
    wide_at = jnp.stack(ranges)
    proj_at = jnp.stack([512 * core, 512 * (1 - core)])

    def exchange(array):
        return lax.all_to_all(
            array.reshape(16, F, D), ("z", "yl"), split_axis=0, concat_axis=0, tiled=True
        ).reshape(P_SIZE, D)

    def both_rows(mine, theirs):
        came = lax.ppermute(theirs, "yl", [(0, 1), (1, 0)])
        return jnp.where(y_lo == 0, jnp.concatenate([mine, came]), jnp.concatenate([came, mine]))

    proj_part = lax.dynamic_slice(spatial_proj, (0, proj_at[0]), (ROWS, PW))
    unit = both_rows(
        jnp.concatenate([proj_part, lax.dynamic_slice(temporal_weight, (0, ranges[0]), (ROWS, WIDE))], axis=1),
        jnp.concatenate([proj_part, lax.dynamic_slice(temporal_weight, (0, ranges[2]), (ROWS, WIDE))], axis=1),
    )
    proj = lax.all_gather(unit[:, :PW], "z", axis=0, tiled=True)
    grad_t = exchange(temporal_grad)
    spatial_out = call(
        forward_kernel, "attend", shape(P_SIZE, D), [VMEM], VMEM, flops=4 * HEADS * 256 ** 3, moved=4 << 20
    )(spatial_qkv)
    ahead, behind = [unit[:, PW:]], [unit[:, PW:]]
    for step in range(1, 4):
        up, down = ahead[-1], behind[-1]
        if step > 1:
            up, down, spatial_out = lax.optimization_barrier((up, down, spatial_out))
        ahead.append(along_z(up, -1))
        behind.append(along_z(down, 1))
    units = ahead + [along_z(after(ahead[-1], behind[-1]), -1)] + behind[:0:-1]
    came = [
        along_plane(jnp.concatenate([units[index] for index in share]), *step) for share, step in zip(SHARE, STEPS)
    ]

    weight_mine = placed("place_mine", z_at, units, [(index,) for index in range(Z)])
    weight_other = placed("place_other", z_at, came, SHARE)

    proj = after(proj, units[4])
    proj_mate = across_cores(proj)
    spatial_mate = across_cores(spatial_out)
    block_out = call(
        block_kernel, "block", shape(P_SIZE, D), [SMEM] + [VMEM] * 4, VMEM, flops=2 * P_SIZE * D * D, moved=5 << 20
    )(proj_at, after(hidden_in, weight_mine, weight_other), spatial_out, proj, proj_mate)
    block_t = exchange(block_out)
    block_mate = across_cores(block_t)
    weights = (weight_mine, across_cores(weight_mine), weight_other, across_cores(weight_other))

    through, keep, send = call(
        temporal_kernel, "temporal",
        [shape(P_SIZE, D), shape(P_SIZE, 2 * WIDE), shape(P_SIZE, 2 * WIDE)],
        [SMEM, VMEM, VMEM] + [ANY] * 4, [VMEM] * 3,
        [
            pltpu.VMEM((4, D, WIDE), BF), pltpu.VMEM((P_SIZE, QKV), BF), pltpu.VMEM((P_SIZE, QKV), BF),
            pltpu.SemaphoreType.DMA((4,)),
        ],
        flops=4 * P_SIZE * D * QKV + 10 * HEADS * 256 ** 3, moved=16 << 20, limit=40,
    )(wide_at, block_t, grad_t, *weights)
    returned = exchange(through)

    packed_mate = across_cores(send)
    leave = product("leave", z_at, block_t, block_mate, keep, packed_mate, WIDE, WIDE, SHARE)
    came = [along_plane(part, *step) for part, step in zip(leave[::-1], STEPS[::-1])][::-1]
    stay = product(
        "stay", after(z_at, leave[0]), block_t, block_mate, keep, packed_mate, 0, WIDE, [(index,) for index in range(Z)]
    )
    arrived = {}
    for part, share in zip(came, SHARE):
        for place, index in enumerate(share):
            arrived[index] = part[place * UNIT:(place + 1) * UNIT]
    first = plus(stay[4], arrived[4]), plus(stay[5], arrived[5])
    ahead = along_z(first[0], 1)
    behind = along_z(first[1], -1)
    hidden_grad = plus(after(pair_grad, *first, *came, *stay), returned)
    hidden_mine = lax.dynamic_slice(hidden_grad, (0, proj_at[0]), (P_SIZE, PW))
    hidden_mate = across_cores(lax.dynamic_slice(hidden_grad, (0, proj_at[1]), (P_SIZE, PW)))
    (proj_part,) = product(
        "proj_part", 0 * z_at, spatial_out, spatial_mate, hidden_mine, hidden_mate, 0, PW,
        [tuple(range(Z))]
    )
    proj_sum = lax.psum_scatter(proj_part, "z", scatter_dimension=0, tiled=True)
    spatial_grad = call(
        spatial_kernel, "spatial", shape(P_SIZE, QKV), [SMEM] + [VMEM] * 4, VMEM, [pltpu.VMEM((P_SIZE, D), BF)],
        flops=2 * P_SIZE * D * D + 10 * HEADS * 256 ** 3, moved=8 << 20,
    )(proj_at, spatial_qkv, hidden_grad, proj, proj_mate)
    for up, down in ((3, 6), (2, 7)):
        ahead, behind = lax.optimization_barrier((
            plus(stay[up], arrived[up], ahead), plus(stay[down], arrived[down], behind),
            proj_part if up == 3 else spatial_grad,
        ))[:2]
        ahead = along_z(ahead, 1)
        behind = along_z(behind, -1)
    ahead = along_z(after(plus(stay[1], arrived[1], ahead), behind), 1)
    weight_sum = plus(stay[0], arrived[0], ahead, behind)

    both = jnp.concatenate([weight_sum, proj_sum], axis=1)
    total = lax.dynamic_slice(both, (ROWS * y_lo, 0), (ROWS, WIDE + PW))
    total = plus(total, along_plane(lax.dynamic_slice(both, (ROWS * (1 - y_lo), 0), (ROWS, WIDE + PW)), 1, 1))
    total = plus(total, along_plane(total, 2, 0))
    total = plus(total, along_plane(total, 0, 2))
    beside = lax.ppermute(total, "x", [(0, 1), (1, 0), (2, 3), (3, 2)])
    weight_sums = jnp.concatenate([total[:, :WIDE], beside[:, :WIDE]], axis=1)
    proj_sums = plus(total[:, WIDE:], beside[:, WIDE:])
    weight_grad, proj_grad = call(
        finish_kernel, "finish", [shape(ROWS, QKV), shape(ROWS, D)], [SMEM] * 2 + [VMEM] * 4, [VMEM] * 2, moved=2 << 20,
    )(wide_at, proj_at, weight_sums, across_cores(weight_sums), proj_sums, across_cores(proj_sums))
    return (
        spatial_grad.reshape(1, P_SIZE, QKV),
        hidden_grad.reshape(1, P_SIZE, D),
        proj_grad,
        weight_grad,
    )


def solution(mesh):
    fine = Mesh(mesh.devices.reshape(8, 2, 2, 4, 2), ("z", "yl", "yh", "x", "c"))
    tokens = P(("yh", "x", "c"), ("z", "yl"), None)
    rows = P(("z", "yl"), None)
    return jax.shard_map(
        per_device,
        mesh=fine,
        in_specs=(tokens, tokens, tokens, tokens, rows, rows),
        out_specs=(tokens, tokens, rows, rows),
        check_vma=False,
    )
```

```python
import functools
import math

import jax
import jax.numpy as jnp
from jax import lax
from jax.experimental import pallas as pl
from jax.experimental.pallas import tpu as pltpu
from jax.sharding import Mesh, PartitionSpec as P

HEADS = 16
HEAD_DIM = 72
P_SIZE = 256
D = HEADS * HEAD_DIM
QKV = 3 * D
F = 16
SCALE = HEAD_DIM ** -0.5
EXP2_SCALE = SCALE * math.log2(math.e)
ROWS = 72
UNIT = 2 * ROWS
Z = 8
WIDE = 896
PW = 640
NORM = (16 * 4096) ** -0.5
BF = jnp.bfloat16
F32 = jnp.float32


def wide_start(index):
    return 128 * (7 * index - (index >= 2))


def head_window(head):
    low = head * HEAD_DIM
    start = low // 128 * 128
    stop = -(-(low + HEAD_DIM) // 128) * 128
    return low, start, stop


def lanes_of(head, rows):
    low, start, stop = head_window(head)
    lane = lax.broadcasted_iota(jnp.int32, (rows, stop - start), 1) + start
    return (lane >= low) & (lane < low + HEAD_DIM)


def nt(a, b):
    return lax.dot_general(a, b, (((1,), (1,)), ((), ())), preferred_element_type=F32)


def nn(a, b):
    return lax.dot_general(a, b, (((1,), (0,)), ((), ())), preferred_element_type=F32)


def tn(a, b):
    return lax.dot_general(a, b, (((0,), (0,)), ((), ())), preferred_element_type=F32)


def add_window(tiles, start, stop, value):
    for index in range(start // 128, stop // 128):
        part = value[:, index * 128 - start:(index + 1) * 128 - start]
        tiles[index] = part if index not in tiles else tiles[index] + part


def flush(tiles, ref, base, upto):
    for index in sorted(tiles):
        if (index + 1) * 128 <= upto:
            ref[:, base + index * 128:base + (index + 1) * 128] = tiles.pop(index).astype(BF)


def forward_kernel(qkv_ref, out_ref):
    rows = qkv_ref.shape[0]
    tiles = {}
    for head in range(HEADS):
        low, start, stop = head_window(head)
        keep = lanes_of(head, rows)
        queries = jnp.where(keep, qkv_ref[:, start:stop], 0)
        keys = qkv_ref[:, D + start:D + stop]
        values = jnp.where(keep, qkv_ref[:, 2 * D + start:2 * D + stop], 0)
        powers = jnp.exp2(nt(queries, keys) * EXP2_SCALE)
        probs = powers / jnp.sum(powers, axis=1, keepdims=True)
        add_window(tiles, start, stop, nn(probs.astype(BF), values))
        flush(tiles, out_ref, 0, low + HEAD_DIM)


def backward(masked, qkv_ref, grad_ref, out_ref):
    rows = qkv_ref.shape[0]
    if masked:
        one = lax.broadcasted_iota(jnp.int32, (rows, rows), 0)
        two = lax.broadcasted_iota(jnp.int32, (rows, rows), 1)
        same = ((one ^ two) & (rows // F - 1)) == 0
    tiles_q, tiles_k, tiles_v = {}, {}, {}
    for head in range(HEADS):
        low, start, stop = head_window(head)
        keep = lanes_of(head, rows)
        queries = jnp.where(keep, qkv_ref[:, start:stop], 0)
        keys = jnp.where(keep, qkv_ref[:, D + start:D + stop], 0)
        values = qkv_ref[:, 2 * D + start:2 * D + stop]
        upstream = jnp.where(keep, grad_ref[:, start:stop], 0)
        powers = jnp.exp2(nt(keys, queries) * EXP2_SCALE)
        if masked:
            powers = jnp.where(same, powers, 0.0)
        probs = powers * (1.0 / jnp.sum(powers, axis=0, keepdims=True))
        prob_grad = nt(values, upstream)
        if masked:
            prob_grad = jnp.where(same, prob_grad, 0.0)
        weighted = probs * prob_grad
        centre = jnp.sum(weighted, axis=0, keepdims=True)
        logit_grad = ((weighted - probs * centre) * SCALE).astype(BF)
        add_window(tiles_v, start, stop, nn(probs.astype(BF), upstream))
        add_window(tiles_k, start, stop, nn(logit_grad, queries))
        add_window(tiles_q, start, stop, tn(logit_grad, keys))
        flush(tiles_q, out_ref, 0, low + HEAD_DIM)
        flush(tiles_k, out_ref, D, low + HEAD_DIM)
        flush(tiles_v, out_ref, 2 * D, low + HEAD_DIM)


VMEM = pl.BlockSpec(memory_space=pltpu.VMEM)
SMEM = pl.BlockSpec(memory_space=pltpu.SMEM)
ANY = pl.BlockSpec(memory_space=pl.ANY)


def shape(*dims):
    return jax.ShapeDtypeStruct(dims, BF)


def call(kernel, name, out_shape, in_specs, out_specs, scratch=(), flops=0, moved=0, limit=32):
    return pl.pallas_call(
        kernel,
        out_shape=out_shape,
        in_specs=in_specs,
        out_specs=out_specs,
        scratch_shapes=scratch,
        compiler_params=pltpu.CompilerParams(vmem_limit_bytes=limit << 20),
        cost_estimate=pl.CostEstimate(flops=flops // 1000, bytes_accessed=moved // 1000, transcendentals=0),
        name=name,
    )


def columns(ref, start, width):
    return ref[:, pl.ds(pl.multiple_of(start, 128), width)]


def from_second_tile(value, shared):
    lane = lax.broadcasted_iota(jnp.int32, value.shape, 1)
    return jnp.where((lane < 128) & shared, jnp.zeros_like(value), value)


def block_kernel(at_ref, hidden_ref, out_ref, proj_ref, mate_ref, block_ref):
    for index, weight in enumerate((proj_ref, mate_ref)):
        start = pl.multiple_of(at_ref[index], 128)
        total = columns(hidden_ref, start, PW).astype(F32) + nn(out_ref[...], weight[...])
        block_ref[:, pl.ds(start, PW)] = total.astype(BF)


def temporal_kernel(at_ref, block_ref, grad_ref, w0, w1, w2, w3, through_ref, keep_ref, send_ref, held, qkv, packed, sems):
    copies = [pltpu.make_async_copy(w, held.at[index], sems.at[index]) for index, w in enumerate((w0, w1, w2, w3))]
    for copy in copies:
        copy.start()
    for index, copy in enumerate(copies):
        copy.wait()
        start = pl.multiple_of(at_ref[index], 128)
        qkv[:, pl.ds(start, WIDE)] = nn(block_ref[...], held[index]).astype(BF)
    backward(True, qkv, grad_ref, packed)
    through = None
    for index in range(4):
        part = columns(packed, at_ref[index], WIDE)
        (send_ref if index % 2 else keep_ref)[:, index // 2 * WIDE:(index // 2 + 1) * WIDE] = part
        term = nt(from_second_tile(part, at_ref[index] == wide_start(2)), held[index])
        through = term if through is None else through + term
    through_ref[...] = through.astype(BF)


def spatial_kernel(at_ref, qkv_ref, hidden_ref, proj_ref, mate_ref, out_ref, back):
    total = None
    for index, weight in enumerate((proj_ref, mate_ref)):
        start = at_ref[index]
        term = nt(from_second_tile(columns(hidden_ref, start, PW), start > 0), weight[...])
        total = term if total is None else total + term
    back[...] = total.astype(BF)
    backward(False, qkv_ref, back, out_ref)


def product_kernel(where, column, width, z_ref, left0, left1, right0, right1, *rest):
    outs, lefts, rights, total = rest[:-3], rest[-3], rest[-2], rest[-1]
    lefts[:P_SIZE] = left0[...]
    lefts[P_SIZE:] = left1[...]
    rights[:P_SIZE] = right0[:, column:column + width]
    rights[P_SIZE:] = right1[:, column:column + width]
    total[...] = tn(lefts[...], rights[...]).astype(BF)
    for out, units in zip(outs, where):
        for place, unit in enumerate(units):
            row = pl.multiple_of(lax.rem(z_ref[0] + unit, Z) * UNIT, 16)
            out[place * UNIT:(place + 1) * UNIT, :] = total[pl.ds(row, UNIT), :]


def product(name, z, left0, left1, right0, right1, column, width, where):
    return call(
        functools.partial(product_kernel, where, column, width), name,
        [shape(UNIT * len(units), width) for units in where],
        [SMEM] + [VMEM] * 4, [VMEM] * len(where),
        [pltpu.VMEM((2 * P_SIZE, D), BF), pltpu.VMEM((2 * P_SIZE, width), BF), pltpu.VMEM((D, width), BF)],
        flops=4 * P_SIZE * D * width, moved=6 << 20,
    )(z, left0, left1, right0, right1)


def place_kernel(where, z_ref, *rest):
    parts, out, sems = rest[:len(where)], rest[-2], rest[-1]
    copies = []
    for part, units in zip(parts, where):
        for place, unit in enumerate(units):
            row = pl.multiple_of(lax.rem(z_ref[0] + unit, Z) * UNIT, 16)
            copies.append(pltpu.make_async_copy(
                part.at[pl.ds(place * UNIT, UNIT)], out.at[pl.ds(row, UNIT)], sems.at[len(copies)]))
    for copy in copies:
        copy.start()
    for copy in copies:
        copy.wait()


def placed(name, z, parts, where):
    width = parts[0].shape[1]
    return call(
        functools.partial(place_kernel, where), name, shape(D, width),
        [SMEM] + [ANY] * len(parts), VMEM, [pltpu.SemaphoreType.DMA((Z,))], moved=4 << 20,
    )(z, *parts)


def finish_kernel(at_ref, pat_ref, mine_ref, mate_ref, mine_p, mate_p, weight_ref, proj_ref):
    for index in range(4):
        source = mate_ref if index % 2 else mine_ref
        part = source[:, index // 2 * WIDE:(index // 2 + 1) * WIDE]
        start = pl.multiple_of(at_ref[index], 128)
        weight_ref[:, pl.ds(start, WIDE)] = (part.astype(F32) * NORM).astype(BF)
    for index, source in enumerate((mine_p, mate_p)):
        start = pl.multiple_of(pat_ref[index], 128)
        proj_ref[:, pl.ds(start, PW)] = (source[...].astype(F32) * NORM).astype(BF)


def along_z(array, by):
    return lax.ppermute(array, "z", [(index, (index + by) % Z) for index in range(Z)])


def along_plane(array, by_x, by_y):
    pairs = []
    for lo in range(2):
        for hi in range(2):
            for x in range(4):
                y = (2 * hi + lo + by_y) % 4
                pairs.append(((lo * 2 + hi) * 4 + x, (y % 2 * 2 + y // 2) * 4 + (x + by_x) % 4))
    return lax.ppermute(array, ("yl", "yh", "x"), pairs)


def across_cores(array):
    return lax.ppermute(array, "c", [(0, 1), (1, 0)])


def after(value, *others):
    return lax.optimization_barrier((value, *others))[0]


def plus(one, *more):
    total = one.astype(F32)
    for value in more:
        total = total + value.astype(F32)
    return total.astype(BF)


SHARE = ((0, 1), (7, 2), (6, 3), (5, 4))
STEPS = ((1, 0), (-1, 0), (0, 1), (0, -1))


def per_device(hidden_in, spatial_qkv, temporal_grad, pair_grad, spatial_proj, temporal_weight):
    z, y_lo, x, core = (lax.axis_index(name) for name in ("z", "yl", "x", "c"))
    odd = (x + y_lo) % 2
    z_at = z.reshape(1)
    hidden_in = hidden_in.reshape(P_SIZE, D)
    spatial_qkv = spatial_qkv.reshape(P_SIZE, QKV)
    pair_grad = pair_grad.reshape(P_SIZE, D)

    ranges = [wide_start(2 * parity + side) for parity in (odd, 1 - odd) for side in (core, 1 - core)]
    wide_at = jnp.stack(ranges)
    proj_at = jnp.stack([512 * core, 512 * (1 - core)])

    def exchange(array):
        return lax.all_to_all(
            array.reshape(16, F, D), ("z", "yl"), split_axis=0, concat_axis=0, tiled=True
        ).reshape(P_SIZE, D)

    def both_rows(mine, theirs):
        came = lax.ppermute(theirs, "yl", [(0, 1), (1, 0)])
        return jnp.where(y_lo == 0, jnp.concatenate([mine, came]), jnp.concatenate([came, mine]))

    proj_part = lax.dynamic_slice(spatial_proj, (0, proj_at[0]), (ROWS, PW))
    unit = both_rows(
        jnp.concatenate([proj_part, lax.dynamic_slice(temporal_weight, (0, ranges[0]), (ROWS, WIDE))], axis=1),
        jnp.concatenate([proj_part, lax.dynamic_slice(temporal_weight, (0, ranges[2]), (ROWS, WIDE))], axis=1),
    )
    proj = lax.all_gather(unit[:, :PW], "z", axis=0, tiled=True)
    grad_t = exchange(temporal_grad)
    spatial_out = call(
        forward_kernel, "attend", shape(P_SIZE, D), [VMEM], VMEM, flops=4 * HEADS * 256 ** 3, moved=4 << 20
    )(spatial_qkv)
    ahead, behind = [unit[:, PW:]], [unit[:, PW:]]
    for step in range(1, 4):
        up, down = ahead[-1], behind[-1]
        if step > 1:
            up, down, spatial_out = lax.optimization_barrier((up, down, spatial_out))
        ahead.append(along_z(up, -1))
        behind.append(along_z(down, 1))
    units = ahead + [along_z(after(ahead[-1], behind[-1]), -1)] + behind[:0:-1]
    came = [
        along_plane(jnp.concatenate([units[index] for index in share]), *step) for share, step in zip(SHARE, STEPS)
    ]

    weight_mine = placed("place_mine", z_at, units, [(index,) for index in range(Z)])
    weight_other = placed("place_other", z_at, came, SHARE)

    proj = after(proj, units[4])
    proj_mate = across_cores(proj)
    spatial_mate = across_cores(spatial_out)
    block_out = call(
        block_kernel, "block", shape(P_SIZE, D), [SMEM] + [VMEM] * 4, VMEM, flops=2 * P_SIZE * D * D, moved=5 << 20, limit=60
    )(proj_at, after(hidden_in, weight_mine, weight_other), spatial_out, proj, proj_mate)
    block_t = exchange(block_out)
    block_mate = across_cores(block_t)
    weights = (weight_mine, across_cores(weight_mine), weight_other, across_cores(weight_other))

    through, keep, send = call(
        temporal_kernel, "temporal",
        [shape(P_SIZE, D), shape(P_SIZE, 2 * WIDE), shape(P_SIZE, 2 * WIDE)],
        [SMEM, VMEM, VMEM] + [ANY] * 4, [VMEM] * 3,
        [
            pltpu.VMEM((4, D, WIDE), BF), pltpu.VMEM((P_SIZE, QKV), BF), pltpu.VMEM((P_SIZE, QKV), BF),
            pltpu.SemaphoreType.DMA((4,)),
        ],
        flops=4 * P_SIZE * D * QKV + 10 * HEADS * 256 ** 3, moved=16 << 20, limit=40,
    )(wide_at, block_t, grad_t, *weights)
    returned = exchange(through)

    packed_mate = across_cores(send)
    leave = product("leave", z_at, block_t, block_mate, keep, packed_mate, WIDE, WIDE, SHARE)
    came = [along_plane(part, *step) for part, step in zip(leave[::-1], STEPS[::-1])][::-1]
    stay = product(
        "stay", after(z_at, leave[0]), block_t, block_mate, keep, packed_mate, 0, WIDE, [(index,) for index in range(Z)]
    )
    hidden_grad = plus(after(pair_grad, *stay, came[3], came[2]), returned)
    hidden_mine = lax.dynamic_slice(hidden_grad, (0, proj_at[0]), (P_SIZE, PW))
    hidden_mate = across_cores(lax.dynamic_slice(hidden_grad, (0, proj_at[1]), (P_SIZE, PW)))
    (proj_part,) = product(
        "proj_part", 0 * z_at, spatial_out, spatial_mate, hidden_mine, hidden_mate, 0, PW,
        [tuple(range(Z))]
    )
    arrived = {}
    for part, share in zip(came, SHARE):
        for place, index in enumerate(share):
            arrived[index] = part[place * UNIT:(place + 1) * UNIT]
    proj_sum = lax.psum_scatter(proj_part, "z", scatter_dimension=0, tiled=True)
    first = plus(stay[4], arrived[4]), plus(stay[5], arrived[5])
    ahead = along_z(first[0], 1)
    behind = along_z(first[1], -1)
    spatial_grad = call(
        spatial_kernel, "spatial", shape(P_SIZE, QKV), [SMEM] + [VMEM] * 4, VMEM, [pltpu.VMEM((P_SIZE, D), BF)],
        flops=2 * P_SIZE * D * D + 10 * HEADS * 256 ** 3, moved=8 << 20,
    )(proj_at, spatial_qkv, hidden_grad, proj, proj_mate)
    for up, down in ((3, 6), (2, 7)):
        ahead, behind = lax.optimization_barrier((
            plus(stay[up], arrived[up], ahead), plus(stay[down], arrived[down], behind),
            proj_part if up == 3 else spatial_grad,
        ))[:2]
        ahead = along_z(ahead, 1)
        behind = along_z(behind, -1)
    ahead = along_z(after(plus(stay[1], arrived[1], ahead), behind), 1)
    weight_sum = plus(stay[0], arrived[0], ahead, behind)

    both = jnp.concatenate([weight_sum, proj_sum], axis=1)
    here = lax.dynamic_slice(both, (ROWS * y_lo, 0), (ROWS, WIDE + PW))
    there = lax.dynamic_slice(both, (ROWS * (1 - y_lo), 0), (ROWS, WIDE + PW))
    total = plus(here, along_plane(there, 1, 1), along_plane(there, -1, -1), along_plane(here, 0, 2))
    total = plus(total, along_plane(total, 2, 0))
    beside = lax.ppermute(total, "x", [(0, 1), (1, 0), (2, 3), (3, 2)])
    weight_sums = jnp.concatenate([total[:, :WIDE], beside[:, :WIDE]], axis=1)
    proj_sums = plus(total[:, WIDE:], beside[:, WIDE:])
    weight_grad, proj_grad = call(
        finish_kernel, "finish", [shape(ROWS, QKV), shape(ROWS, D)], [SMEM] * 2 + [VMEM] * 4, [VMEM] * 2, moved=2 << 20,
    )(wide_at, proj_at, weight_sums, across_cores(weight_sums), proj_sums, across_cores(proj_sums))
    return (
        spatial_grad.reshape(1, P_SIZE, QKV),
        hidden_grad.reshape(1, P_SIZE, D),
        proj_grad,
        weight_grad,
    )


def solution(mesh):
    fine = Mesh(mesh.devices.reshape(8, 2, 2, 4, 2), ("z", "yl", "yh", "x", "c"))
    tokens = P(("yh", "x", "c"), ("z", "yl"), None)
    rows = P(("z", "yl"), None)
    return jax.shard_map(
        per_device,
        mesh=fine,
        in_specs=(tokens, tokens, tokens, tokens, rows, rows),
        out_specs=(tokens, tokens, rows, rows),
        check_vma=False,
    )
```

```python
import functools
import math

import jax
import jax.numpy as jnp
from jax import lax
from jax.experimental import pallas as pl
from jax.experimental.pallas import tpu as pltpu
from jax.sharding import Mesh, PartitionSpec as P

HEADS = 16
HEAD_DIM = 72
P_SIZE = 256
D = HEADS * HEAD_DIM
QKV = 3 * D
F = 16
SCALE = HEAD_DIM ** -0.5
EXP2_SCALE = SCALE * math.log2(math.e)
ROWS = 72
UNIT = 2 * ROWS
Z = 8
WIDE = 896
PW = 640
NORM = (16 * 4096) ** -0.5
BF = jnp.bfloat16
F32 = jnp.float32


def wide_start(index):
    return 128 * (7 * index - (index >= 2))


def head_window(head):
    low = head * HEAD_DIM
    start = low // 128 * 128
    stop = -(-(low + HEAD_DIM) // 128) * 128
    return low, start, stop


def lanes_of(head, rows):
    low, start, stop = head_window(head)
    lane = lax.broadcasted_iota(jnp.int32, (rows, stop - start), 1) + start
    return (lane >= low) & (lane < low + HEAD_DIM)


def nt(a, b):
    return lax.dot_general(a, b, (((1,), (1,)), ((), ())), preferred_element_type=F32)


def nn(a, b):
    return lax.dot_general(a, b, (((1,), (0,)), ((), ())), preferred_element_type=F32)


def tn(a, b):
    return lax.dot_general(a, b, (((0,), (0,)), ((), ())), preferred_element_type=F32)


def add_window(tiles, start, stop, value):
    for index in range(start // 128, stop // 128):
        part = value[:, index * 128 - start:(index + 1) * 128 - start]
        tiles[index] = part if index not in tiles else tiles[index] + part


def flush(tiles, ref, base, upto):
    for index in sorted(tiles):
        if (index + 1) * 128 <= upto:
            ref[:, base + index * 128:base + (index + 1) * 128] = tiles.pop(index).astype(BF)


def forward_kernel(qkv_ref, out_ref):
    rows = qkv_ref.shape[0]
    tiles = {}
    for head in range(HEADS):
        low, start, stop = head_window(head)
        keep = lanes_of(head, rows)
        queries = jnp.where(keep, qkv_ref[:, start:stop], 0)
        keys = qkv_ref[:, D + start:D + stop]
        values = jnp.where(keep, qkv_ref[:, 2 * D + start:2 * D + stop], 0)
        powers = jnp.exp2(nt(queries, keys) * EXP2_SCALE)
        probs = powers / jnp.sum(powers, axis=1, keepdims=True)
        add_window(tiles, start, stop, nn(probs.astype(BF), values))
        flush(tiles, out_ref, 0, low + HEAD_DIM)


def backward(masked, qkv_ref, grad_ref, out_ref):
    rows = qkv_ref.shape[0]
    if masked:
        one = lax.broadcasted_iota(jnp.int32, (rows, rows), 0)
        two = lax.broadcasted_iota(jnp.int32, (rows, rows), 1)
        same = ((one ^ two) & (rows // F - 1)) == 0
    tiles_q, tiles_k, tiles_v = {}, {}, {}
    for head in range(HEADS):
        low, start, stop = head_window(head)
        keep = lanes_of(head, rows)
        queries = jnp.where(keep, qkv_ref[:, start:stop], 0)
        keys = jnp.where(keep, qkv_ref[:, D + start:D + stop], 0)
        values = qkv_ref[:, 2 * D + start:2 * D + stop]
        upstream = jnp.where(keep, grad_ref[:, start:stop], 0)
        powers = jnp.exp2(nt(keys, queries) * EXP2_SCALE)
        if masked:
            powers = jnp.where(same, powers, 0.0)
        probs = powers * (1.0 / jnp.sum(powers, axis=0, keepdims=True))
        prob_grad = nt(values, upstream)
        if masked:
            prob_grad = jnp.where(same, prob_grad, 0.0)
        weighted = probs * prob_grad
        centre = jnp.sum(weighted, axis=0, keepdims=True)
        logit_grad = ((weighted - probs * centre) * SCALE).astype(BF)
        add_window(tiles_v, start, stop, nn(probs.astype(BF), upstream))
        add_window(tiles_k, start, stop, nn(logit_grad, queries))
        add_window(tiles_q, start, stop, tn(logit_grad, keys))
        flush(tiles_q, out_ref, 0, low + HEAD_DIM)
        flush(tiles_k, out_ref, D, low + HEAD_DIM)
        flush(tiles_v, out_ref, 2 * D, low + HEAD_DIM)


VMEM = pl.BlockSpec(memory_space=pltpu.VMEM)
SMEM = pl.BlockSpec(memory_space=pltpu.SMEM)
ANY = pl.BlockSpec(memory_space=pl.ANY)


def shape(*dims):
    return jax.ShapeDtypeStruct(dims, BF)


def call(kernel, name, out_shape, in_specs, out_specs, scratch=(), flops=0, moved=0, limit=32):
    return pl.pallas_call(
        kernel,
        out_shape=out_shape,
        in_specs=in_specs,
        out_specs=out_specs,
        scratch_shapes=scratch,
        compiler_params=pltpu.CompilerParams(vmem_limit_bytes=limit << 20),
        cost_estimate=pl.CostEstimate(flops=flops // 1000, bytes_accessed=moved // 1000, transcendentals=0),
        name=name,
    )


def columns(ref, start, width):
    return ref[:, pl.ds(pl.multiple_of(start, 128), width)]


def from_second_tile(value, shared):
    lane = lax.broadcasted_iota(jnp.int32, value.shape, 1)
    return jnp.where((lane < 128) & shared, jnp.zeros_like(value), value)


def block_kernel(at_ref, hidden_ref, out_ref, proj_ref, mate_ref, block_ref):
    for index, weight in enumerate((proj_ref, mate_ref)):
        start = pl.multiple_of(at_ref[index], 128)
        total = columns(hidden_ref, start, PW).astype(F32) + nn(out_ref[...], weight[...])
        block_ref[:, pl.ds(start, PW)] = total.astype(BF)


def temporal_kernel(at_ref, block_ref, grad_ref, w0, w1, w2, w3, through_ref, keep_ref, send_ref, held, qkv, packed, sems):
    copies = [pltpu.make_async_copy(w, held.at[index], sems.at[index]) for index, w in enumerate((w0, w1, w2, w3))]
    for copy in copies:
        copy.start()
    for index, copy in enumerate(copies):
        copy.wait()
        start = pl.multiple_of(at_ref[index], 128)
        qkv[:, pl.ds(start, WIDE)] = nn(block_ref[...], held[index]).astype(BF)
    backward(True, qkv, grad_ref, packed)
    through = None
    for index in range(4):
        part = columns(packed, at_ref[index], WIDE)
        (send_ref if index % 2 else keep_ref)[:, index // 2 * WIDE:(index // 2 + 1) * WIDE] = part
        term = nt(from_second_tile(part, at_ref[index] == wide_start(2)), held[index])
        through = term if through is None else through + term
    through_ref[...] = through.astype(BF)


def spatial_kernel(at_ref, qkv_ref, hidden_ref, proj_ref, mate_ref, out_ref, back):
    total = None
    for index, weight in enumerate((proj_ref, mate_ref)):
        start = at_ref[index]
        term = nt(from_second_tile(columns(hidden_ref, start, PW), start > 0), weight[...])
        total = term if total is None else total + term
    back[...] = total.astype(BF)
    backward(False, qkv_ref, back, out_ref)


def product_kernel(where, column, width, z_ref, left0, left1, right0, right1, *rest):
    outs, lefts, rights, total = rest[:-3], rest[-3], rest[-2], rest[-1]
    lefts[:P_SIZE] = left0[...]
    lefts[P_SIZE:] = left1[...]
    rights[:P_SIZE] = right0[:, column:column + width]
    rights[P_SIZE:] = right1[:, column:column + width]
    total[...] = tn(lefts[...], rights[...]).astype(BF)
    for out, units in zip(outs, where):
        for place, unit in enumerate(units):
            row = pl.multiple_of(lax.rem(z_ref[0] + unit, Z) * UNIT, 16)
            out[place * UNIT:(place + 1) * UNIT, :] = total[pl.ds(row, UNIT), :]


def product(name, z, left0, left1, right0, right1, column, width, where):
    return call(
        functools.partial(product_kernel, where, column, width), name,
        [shape(UNIT * len(units), width) for units in where],
        [SMEM] + [VMEM] * 4, [VMEM] * len(where),
        [pltpu.VMEM((2 * P_SIZE, D), BF), pltpu.VMEM((2 * P_SIZE, width), BF), pltpu.VMEM((D, width), BF)],
        flops=4 * P_SIZE * D * width, moved=6 << 20,
    )(z, left0, left1, right0, right1)


def place_kernel(where, z_ref, *rest):
    parts, out, sems = rest[:len(where)], rest[-2], rest[-1]
    copies = []
    for part, units in zip(parts, where):
        for place, unit in enumerate(units):
            row = pl.multiple_of(lax.rem(z_ref[0] + unit, Z) * UNIT, 16)
            copies.append(pltpu.make_async_copy(
                part.at[pl.ds(place * UNIT, UNIT)], out.at[pl.ds(row, UNIT)], sems.at[len(copies)]))
    for copy in copies:
        copy.start()
    for copy in copies:
        copy.wait()


def placed(name, z, parts, where):
    width = parts[0].shape[1]
    return call(
        functools.partial(place_kernel, where), name, shape(D, width),
        [SMEM] + [ANY] * len(parts), VMEM, [pltpu.SemaphoreType.DMA((Z,))], moved=4 << 20,
    )(z, *parts)


def finish_kernel(at_ref, pat_ref, mine_ref, mate_ref, mine_p, mate_p, weight_ref, proj_ref):
    for index in range(4):
        source = mate_ref if index % 2 else mine_ref
        part = source[:, index // 2 * WIDE:(index // 2 + 1) * WIDE]
        start = pl.multiple_of(at_ref[index], 128)
        weight_ref[:, pl.ds(start, WIDE)] = (part.astype(F32) * NORM).astype(BF)
    for index, source in enumerate((mine_p, mate_p)):
        start = pl.multiple_of(pat_ref[index], 128)
        proj_ref[:, pl.ds(start, PW)] = (source[...].astype(F32) * NORM).astype(BF)


def along_z(array, by):
    return lax.ppermute(array, "z", [(index, (index + by) % Z) for index in range(Z)])


def along_plane(array, by_x, by_y):
    pairs = []
    for lo in range(2):
        for hi in range(2):
            for x in range(4):
                y = (2 * hi + lo + by_y) % 4
                pairs.append(((lo * 2 + hi) * 4 + x, (y % 2 * 2 + y // 2) * 4 + (x + by_x) % 4))
    return lax.ppermute(array, ("yl", "yh", "x"), pairs)


def across_cores(array):
    return lax.ppermute(array, "c", [(0, 1), (1, 0)])


def after(value, *others):
    return lax.optimization_barrier((value, *others))[0]


def plus(one, *more):
    total = one.astype(F32)
    for value in more:
        total = total + value.astype(F32)
    return total.astype(BF)


SHARE = ((0, 1), (7, 2), (6, 3), (5, 4))
STEPS = ((1, 0), (-1, 0), (0, 1), (0, -1))
DUE = ((5, 4), (6, 3), (7, 2), (0, 1))


def per_device(hidden_in, spatial_qkv, temporal_grad, pair_grad, spatial_proj, temporal_weight):
    z, y_lo, x, core = (lax.axis_index(name) for name in ("z", "yl", "x", "c"))
    odd = (x + y_lo) % 2
    z_at = z.reshape(1)
    hidden_in = hidden_in.reshape(P_SIZE, D)
    spatial_qkv = spatial_qkv.reshape(P_SIZE, QKV)
    pair_grad = pair_grad.reshape(P_SIZE, D)

    ranges = [wide_start(2 * parity + side) for parity in (odd, 1 - odd) for side in (core, 1 - core)]
    wide_at = jnp.stack(ranges)
    proj_at = jnp.stack([512 * core, 512 * (1 - core)])

    def exchange(array):
        return lax.all_to_all(
            array.reshape(16, F, D), ("z", "yl"), split_axis=0, concat_axis=0, tiled=True
        ).reshape(P_SIZE, D)

    def both_rows(mine, theirs):
        came = lax.ppermute(theirs, "yl", [(0, 1), (1, 0)])
        return jnp.where(y_lo == 0, jnp.concatenate([mine, came]), jnp.concatenate([came, mine]))

    proj_part = lax.dynamic_slice(spatial_proj, (0, proj_at[0]), (ROWS, PW))
    unit = both_rows(
        jnp.concatenate([proj_part, lax.dynamic_slice(temporal_weight, (0, ranges[0]), (ROWS, WIDE))], axis=1),
        jnp.concatenate([proj_part, lax.dynamic_slice(temporal_weight, (0, ranges[2]), (ROWS, WIDE))], axis=1),
    )
    proj = lax.all_gather(unit[:, :PW], "z", axis=0, tiled=True)
    grad_t = exchange(temporal_grad)
    spatial_out = call(
        forward_kernel, "attend", shape(P_SIZE, D), [VMEM], VMEM, flops=4 * HEADS * 256 ** 3, moved=4 << 20
    )(spatial_qkv)
    ahead, behind = [unit[:, PW:]], [unit[:, PW:]]
    for step in range(1, 4):
        up, down = ahead[-1], behind[-1]
        if step > 1:
            up, down, spatial_out = lax.optimization_barrier((up, down, spatial_out))
        ahead.append(along_z(up, -1))
        behind.append(along_z(down, 1))
    units = ahead + [along_z(after(ahead[-1], behind[-1]), -1)] + behind[:0:-1]
    came = [
        along_plane(jnp.concatenate([units[index] for index in share]), *step) for share, step in zip(SHARE, STEPS)
    ]

    weight_mine = placed("place_mine", z_at, units, [(index,) for index in range(Z)])
    weight_other = placed("place_other", z_at, came, SHARE)

    proj = after(proj, units[4])
    proj_mate = across_cores(proj)
    spatial_mate = across_cores(spatial_out)
    block_out = call(
        block_kernel, "block", shape(P_SIZE, D), [SMEM] + [VMEM] * 4, VMEM, flops=2 * P_SIZE * D * D, moved=5 << 20, limit=60
    )(proj_at, after(hidden_in, weight_mine, weight_other), spatial_out, proj, proj_mate)
    block_t = exchange(block_out)
    block_mate = across_cores(block_t)
    weights = (weight_mine, across_cores(weight_mine), weight_other, across_cores(weight_other))

    through, keep, send = call(
        temporal_kernel, "temporal",
        [shape(P_SIZE, D), shape(P_SIZE, 2 * WIDE), shape(P_SIZE, 2 * WIDE)],
        [SMEM, VMEM, VMEM] + [ANY] * 4, [VMEM] * 3,
        [
            pltpu.VMEM((4, D, WIDE), BF), pltpu.VMEM((P_SIZE, QKV), BF), pltpu.VMEM((P_SIZE, QKV), BF),
            pltpu.SemaphoreType.DMA((4,)),
        ],
        flops=4 * P_SIZE * D * QKV + 10 * HEADS * 256 ** 3, moved=16 << 20, limit=40,
    )(wide_at, block_t, grad_t, *weights)
    returned = exchange(through)

    packed_mate = across_cores(send)
    leave = product("leave", z_at, block_t, block_mate, keep, packed_mate, WIDE, WIDE, DUE)
    came = [along_plane(part, *step) for part, step in zip(leave, STEPS)]
    stay = product(
        "stay", after(z_at, leave[0]), block_t, block_mate, keep, packed_mate, 0, WIDE, [(index,) for index in range(Z)]
    )
    hidden_grad = plus(after(pair_grad, *stay, came[0], came[1]), returned)
    hidden_mine = lax.dynamic_slice(hidden_grad, (0, proj_at[0]), (P_SIZE, PW))
    hidden_mate = across_cores(lax.dynamic_slice(hidden_grad, (0, proj_at[1]), (P_SIZE, PW)))
    (proj_part,) = product(
        "proj_part", 0 * z_at, spatial_out, spatial_mate, hidden_mine, hidden_mate, 0, PW,
        [tuple(range(Z))]
    )
    arrived = {}
    for part, share in zip(came, DUE):
        for place, index in enumerate(share):
            arrived[index] = part[place * UNIT:(place + 1) * UNIT]
    proj_sum = lax.psum_scatter(proj_part, "z", scatter_dimension=0, tiled=True)
    first = plus(stay[4], arrived[4]), plus(stay[5], arrived[5])
    ahead = along_z(first[0], 1)
    behind = along_z(first[1], -1)
    spatial_grad = call(
        spatial_kernel, "spatial", shape(P_SIZE, QKV), [SMEM] + [VMEM] * 4, VMEM, [pltpu.VMEM((P_SIZE, D), BF)],
        flops=2 * P_SIZE * D * D + 10 * HEADS * 256 ** 3, moved=8 << 20,
    )(proj_at, spatial_qkv, hidden_grad, proj, proj_mate)
    for up, down in ((3, 6), (2, 7)):
        ahead, behind = lax.optimization_barrier((
            plus(stay[up], arrived[up], ahead), plus(stay[down], arrived[down], behind),
            proj_part if up == 3 else spatial_grad,
        ))[:2]
        ahead = along_z(ahead, 1)
        behind = along_z(behind, -1)
    ahead = along_z(after(plus(stay[1], arrived[1], ahead), behind), 1)
    weight_sum = plus(stay[0], arrived[0], ahead, behind)

    both = jnp.concatenate([weight_sum, proj_sum], axis=1)
    here = lax.dynamic_slice(both, (ROWS * y_lo, 0), (ROWS, WIDE + PW))
    there = lax.dynamic_slice(both, (ROWS * (1 - y_lo), 0), (ROWS, WIDE + PW))
    total = plus(here, along_plane(there, 1, 1), along_plane(there, -1, -1), along_plane(here, 0, 2))
    total = plus(total, along_plane(total, 2, 0))
    beside = lax.ppermute(total, "x", [(0, 1), (1, 0), (2, 3), (3, 2)])
    weight_sums = jnp.concatenate([total[:, :WIDE], beside[:, :WIDE]], axis=1)
    proj_sums = plus(total[:, WIDE:], beside[:, WIDE:])
    weight_grad, proj_grad = call(
        finish_kernel, "finish", [shape(ROWS, QKV), shape(ROWS, D)], [SMEM] * 2 + [VMEM] * 4, [VMEM] * 2, moved=2 << 20,
    )(wide_at, proj_at, weight_sums, across_cores(weight_sums), proj_sums, across_cores(proj_sums))
    return (
        spatial_grad.reshape(1, P_SIZE, QKV),
        hidden_grad.reshape(1, P_SIZE, D),
        proj_grad,
        weight_grad,
    )


def solution(mesh):
    fine = Mesh(mesh.devices.reshape(8, 2, 2, 4, 2), ("z", "yl", "yh", "x", "c"))
    tokens = P(("yh", "x", "c"), ("z", "yl"), None)
    rows = P(("z", "yl"), None)
    return jax.shard_map(
        per_device,
        mesh=fine,
        in_specs=(tokens, tokens, tokens, tokens, rows, rows),
        out_specs=(tokens, tokens, rows, rows),
        check_vma=False,
    )
```

```python
import functools
import math

import jax
import jax.numpy as jnp
from jax import lax
from jax.experimental import pallas as pl
from jax.experimental.pallas import tpu as pltpu
from jax.sharding import Mesh, PartitionSpec as P

HEADS = 16
HEAD_DIM = 72
P_SIZE = 256
D = HEADS * HEAD_DIM
QKV = 3 * D
F = 16
SCALE = HEAD_DIM ** -0.5
EXP2_SCALE = SCALE * math.log2(math.e)
ROWS = 72
UNIT = 2 * ROWS
Z = 8
WIDE = 896
PW = 640
NORM = (16 * 4096) ** -0.5
BF = jnp.bfloat16
F32 = jnp.float32


def wide_start(index):
    return 128 * (7 * index - (index >= 2))


def head_window(head):
    low = head * HEAD_DIM
    start = low // 128 * 128
    stop = -(-(low + HEAD_DIM) // 128) * 128
    return low, start, stop


def lanes_of(head, rows):
    low, start, stop = head_window(head)
    lane = lax.broadcasted_iota(jnp.int32, (rows, stop - start), 1) + start
    return (lane >= low) & (lane < low + HEAD_DIM)


def nt(a, b):
    return lax.dot_general(a, b, (((1,), (1,)), ((), ())), preferred_element_type=F32)


def nn(a, b):
    return lax.dot_general(a, b, (((1,), (0,)), ((), ())), preferred_element_type=F32)


def tn(a, b):
    return lax.dot_general(a, b, (((0,), (0,)), ((), ())), preferred_element_type=F32)


def add_window(tiles, start, stop, value):
    for index in range(start // 128, stop // 128):
        part = value[:, index * 128 - start:(index + 1) * 128 - start]
        tiles[index] = part if index not in tiles else tiles[index] + part


def flush(tiles, ref, base, upto):
    for index in sorted(tiles):
        if (index + 1) * 128 <= upto:
            ref[:, base + index * 128:base + (index + 1) * 128] = tiles.pop(index).astype(BF)


def in_range(total):
    return jnp.where(total > 2.0 ** 64, 2.0 ** -32, 1.0)


def forward_kernel(qkv_ref, out_ref):
    rows = qkv_ref.shape[0]
    tiles = {}
    for head in range(HEADS):
        low, start, stop = head_window(head)
        keep = lanes_of(head, rows)
        queries = jnp.where(keep, qkv_ref[:, start:stop], 0)
        keys = qkv_ref[:, D + start:D + stop]
        values = jnp.where(keep, qkv_ref[:, 2 * D + start:2 * D + stop], 0)
        powers = jnp.exp2(nt(queries, keys) * EXP2_SCALE)
        total = jnp.sum(powers, axis=1, keepdims=True)
        level = in_range(total)
        probs = powers * level / (total * level)
        add_window(tiles, start, stop, nn(probs.astype(BF), values))
        flush(tiles, out_ref, 0, low + HEAD_DIM)


def backward(masked, qkv_ref, grad_ref, out_ref):
    rows = qkv_ref.shape[0]
    if masked:
        one = lax.broadcasted_iota(jnp.int32, (rows, rows), 0)
        two = lax.broadcasted_iota(jnp.int32, (rows, rows), 1)
        same = ((one ^ two) & (rows // F - 1)) == 0
    tiles_q, tiles_k, tiles_v = {}, {}, {}
    for head in range(HEADS):
        low, start, stop = head_window(head)
        keep = lanes_of(head, rows)
        queries = jnp.where(keep, qkv_ref[:, start:stop], 0)
        keys = jnp.where(keep, qkv_ref[:, D + start:D + stop], 0)
        values = qkv_ref[:, 2 * D + start:2 * D + stop]
        upstream = jnp.where(keep, grad_ref[:, start:stop], 0)
        powers = jnp.exp2(nt(keys, queries) * EXP2_SCALE)
        if masked:
            powers = jnp.where(same, powers, 0.0)
        total = jnp.sum(powers, axis=0, keepdims=True)
        level = in_range(total)
        probs = powers * level * (1.0 / (total * level))
        prob_grad = nt(values, upstream)
        if masked:
            prob_grad = jnp.where(same, prob_grad, 0.0)
        weighted = probs * prob_grad
        centre = jnp.sum(weighted, axis=0, keepdims=True)
        logit_grad = ((weighted - probs * centre) * SCALE).astype(BF)
        add_window(tiles_v, start, stop, nn(probs.astype(BF), upstream))
        add_window(tiles_k, start, stop, nn(logit_grad, queries))
        add_window(tiles_q, start, stop, tn(logit_grad, keys))
        flush(tiles_q, out_ref, 0, low + HEAD_DIM)
        flush(tiles_k, out_ref, D, low + HEAD_DIM)
        flush(tiles_v, out_ref, 2 * D, low + HEAD_DIM)


VMEM = pl.BlockSpec(memory_space=pltpu.VMEM)
SMEM = pl.BlockSpec(memory_space=pltpu.SMEM)
ANY = pl.BlockSpec(memory_space=pl.ANY)


def shape(*dims):
    return jax.ShapeDtypeStruct(dims, BF)


def call(kernel, name, out_shape, in_specs, out_specs, scratch=(), flops=0, moved=0, limit=32):
    return pl.pallas_call(
        kernel,
        out_shape=out_shape,
        in_specs=in_specs,
        out_specs=out_specs,
        scratch_shapes=scratch,
        compiler_params=pltpu.CompilerParams(vmem_limit_bytes=limit << 20),
        cost_estimate=pl.CostEstimate(flops=flops // 1000, bytes_accessed=moved // 1000, transcendentals=0),
        name=name,
    )


def columns(ref, start, width):
    return ref[:, pl.ds(pl.multiple_of(start, 128), width)]


def from_second_tile(value, shared):
    lane = lax.broadcasted_iota(jnp.int32, value.shape, 1)
    return jnp.where((lane < 128) & shared, jnp.zeros_like(value), value)


def block_kernel(at_ref, hidden_ref, out_ref, proj_ref, mate_ref, block_ref):
    for index, weight in enumerate((proj_ref, mate_ref)):
        start = pl.multiple_of(at_ref[index], 128)
        total = columns(hidden_ref, start, PW).astype(F32) + nn(out_ref[...], weight[...])
        block_ref[:, pl.ds(start, PW)] = total.astype(BF)


def temporal_kernel(at_ref, block_ref, grad_ref, w0, w1, w2, w3, through_ref, keep_ref, send_ref, held, qkv, packed, sems):
    copies = [pltpu.make_async_copy(w, held.at[index], sems.at[index]) for index, w in enumerate((w0, w1, w2, w3))]
    for copy in copies:
        copy.start()
    for index, copy in enumerate(copies):
        copy.wait()
        start = pl.multiple_of(at_ref[index], 128)
        qkv[:, pl.ds(start, WIDE)] = nn(block_ref[...], held[index]).astype(BF)
    backward(True, qkv, grad_ref, packed)
    through = None
    for index in range(4):
        part = columns(packed, at_ref[index], WIDE)
        (send_ref if index % 2 else keep_ref)[:, index // 2 * WIDE:(index // 2 + 1) * WIDE] = part
        term = nt(from_second_tile(part, at_ref[index] == wide_start(2)), held[index])
        through = term if through is None else through + term
    through_ref[...] = through.astype(BF)


def spatial_kernel(at_ref, qkv_ref, hidden_ref, proj_ref, mate_ref, out_ref, back):
    total = None
    for index, weight in enumerate((proj_ref, mate_ref)):
        start = at_ref[index]
        term = nt(from_second_tile(columns(hidden_ref, start, PW), start > 0), weight[...])
        total = term if total is None else total + term
    back[...] = total.astype(BF)
    backward(False, qkv_ref, back, out_ref)


def product_kernel(where, column, width, z_ref, left0, left1, right0, right1, *rest):
    outs, lefts, rights, total = rest[:-3], rest[-3], rest[-2], rest[-1]
    lefts[:P_SIZE] = left0[...]
    lefts[P_SIZE:] = left1[...]
    rights[:P_SIZE] = right0[:, column:column + width]
    rights[P_SIZE:] = right1[:, column:column + width]
    total[...] = tn(lefts[...], rights[...]).astype(BF)
    for out, units in zip(outs, where):
        for place, unit in enumerate(units):
            row = pl.multiple_of(lax.rem(z_ref[0] + unit, Z) * UNIT, 16)
            out[place * UNIT:(place + 1) * UNIT, :] = total[pl.ds(row, UNIT), :]


def product(name, z, left0, left1, right0, right1, column, width, where):
    return call(
        functools.partial(product_kernel, where, column, width), name,
        [shape(UNIT * len(units), width) for units in where],
        [SMEM] + [VMEM] * 4, [VMEM] * len(where),
        [pltpu.VMEM((2 * P_SIZE, D), BF), pltpu.VMEM((2 * P_SIZE, width), BF), pltpu.VMEM((D, width), BF)],
        flops=4 * P_SIZE * D * width, moved=6 << 20,
    )(z, left0, left1, right0, right1)


def place_kernel(where, z_ref, *rest):
    parts, out, sems = rest[:len(where)], rest[-2], rest[-1]
    copies = []
    for part, units in zip(parts, where):
        for place, unit in enumerate(units):
            row = pl.multiple_of(lax.rem(z_ref[0] + unit, Z) * UNIT, 16)
            copies.append(pltpu.make_async_copy(
                part.at[pl.ds(place * UNIT, UNIT)], out.at[pl.ds(row, UNIT)], sems.at[len(copies)]))
    for copy in copies:
        copy.start()
    for copy in copies:
        copy.wait()


def placed(name, z, parts, where):
    width = parts[0].shape[1]
    return call(
        functools.partial(place_kernel, where), name, shape(D, width),
        [SMEM] + [ANY] * len(parts), VMEM, [pltpu.SemaphoreType.DMA((Z,))], moved=4 << 20,
    )(z, *parts)


def finish_kernel(at_ref, pat_ref, mine_ref, mate_ref, mine_p, mate_p, weight_ref, proj_ref):
    for index in range(4):
        source = mate_ref if index % 2 else mine_ref
        part = source[:, index // 2 * WIDE:(index // 2 + 1) * WIDE]
        start = pl.multiple_of(at_ref[index], 128)
        weight_ref[:, pl.ds(start, WIDE)] = (part.astype(F32) * NORM).astype(BF)
    for index, source in enumerate((mine_p, mate_p)):
        start = pl.multiple_of(pat_ref[index], 128)
        proj_ref[:, pl.ds(start, PW)] = (source[...].astype(F32) * NORM).astype(BF)


def along_z(array, by):
    return lax.ppermute(array, "z", [(index, (index + by) % Z) for index in range(Z)])


def along_plane(array, by_x, by_y):
    pairs = []
    for lo in range(2):
        for hi in range(2):
            for x in range(4):
                y = (2 * hi + lo + by_y) % 4
                pairs.append(((lo * 2 + hi) * 4 + x, (y % 2 * 2 + y // 2) * 4 + (x + by_x) % 4))
    return lax.ppermute(array, ("yl", "yh", "x"), pairs)


def across_cores(array):
    return lax.ppermute(array, "c", [(0, 1), (1, 0)])


def after(value, *others):
    return lax.optimization_barrier((value, *others))[0]


def plus(one, *more):
    total = one.astype(F32)
    for value in more:
        total = total + value.astype(F32)
    return total.astype(BF)


SHARE = ((0, 1), (7, 2), (6, 3), (5, 4))
STEPS = ((1, 0), (-1, 0), (0, 1), (0, -1))
DUE = ((5, 4), (6, 3), (7, 2), (0, 1))


def per_device(hidden_in, spatial_qkv, temporal_grad, pair_grad, spatial_proj, temporal_weight):
    z, y_lo, x, core = (lax.axis_index(name) for name in ("z", "yl", "x", "c"))
    odd = (x + y_lo) % 2
    z_at = z.reshape(1)
    hidden_in = hidden_in.reshape(P_SIZE, D)
    spatial_qkv = spatial_qkv.reshape(P_SIZE, QKV)
    pair_grad = pair_grad.reshape(P_SIZE, D)

    ranges = [wide_start(2 * parity + side) for parity in (odd, 1 - odd) for side in (core, 1 - core)]
    wide_at = jnp.stack(ranges)
    proj_at = jnp.stack([512 * core, 512 * (1 - core)])

    def exchange(array):
        return lax.all_to_all(
            array.reshape(16, F, D), ("z", "yl"), split_axis=0, concat_axis=0, tiled=True
        ).reshape(P_SIZE, D)

    def both_rows(mine, theirs):
        came = lax.ppermute(theirs, "yl", [(0, 1), (1, 0)])
        return jnp.where(y_lo == 0, jnp.concatenate([mine, came]), jnp.concatenate([came, mine]))

    proj_part = lax.dynamic_slice(spatial_proj, (0, proj_at[0]), (ROWS, PW))
    unit = both_rows(
        jnp.concatenate([proj_part, lax.dynamic_slice(temporal_weight, (0, ranges[0]), (ROWS, WIDE))], axis=1),
        jnp.concatenate([proj_part, lax.dynamic_slice(temporal_weight, (0, ranges[2]), (ROWS, WIDE))], axis=1),
    )
    proj = lax.all_gather(unit[:, :PW], "z", axis=0, tiled=True)
    grad_t = exchange(temporal_grad)
    spatial_out = call(
        forward_kernel, "attend", shape(P_SIZE, D), [VMEM], VMEM, flops=4 * HEADS * 256 ** 3, moved=4 << 20
    )(spatial_qkv)
    ahead, behind = [unit[:, PW:]], [unit[:, PW:]]
    for step in range(1, 4):
        up, down = ahead[-1], behind[-1]
        if step > 1:
            up, down, spatial_out = lax.optimization_barrier((up, down, spatial_out))
        ahead.append(along_z(up, -1))
        behind.append(along_z(down, 1))
    units = ahead + [along_z(after(ahead[-1], behind[-1]), -1)] + behind[:0:-1]
    came = [
        along_plane(jnp.concatenate([units[index] for index in share]), *step) for share, step in zip(SHARE, STEPS)
    ]

    weight_mine = placed("place_mine", z_at, units, [(index,) for index in range(Z)])
    weight_other = placed("place_other", z_at, came, SHARE)

    proj = after(proj, units[4])
    proj_mate = across_cores(proj)
    spatial_mate = across_cores(spatial_out)
    block_out = call(
        block_kernel, "block", shape(P_SIZE, D), [SMEM] + [VMEM] * 4, VMEM, flops=2 * P_SIZE * D * D, moved=5 << 20, limit=60
    )(proj_at, after(hidden_in, weight_mine, weight_other), spatial_out, proj, proj_mate)
    block_t = exchange(block_out)
    block_mate = across_cores(block_t)
    weights = (weight_mine, across_cores(weight_mine), weight_other, across_cores(weight_other))

    through, keep, send = call(
        temporal_kernel, "temporal",
        [shape(P_SIZE, D), shape(P_SIZE, 2 * WIDE), shape(P_SIZE, 2 * WIDE)],
        [SMEM, VMEM, VMEM] + [ANY] * 4, [VMEM] * 3,
        [
            pltpu.VMEM((4, D, WIDE), BF), pltpu.VMEM((P_SIZE, QKV), BF), pltpu.VMEM((P_SIZE, QKV), BF),
            pltpu.SemaphoreType.DMA((4,)),
        ],
        flops=4 * P_SIZE * D * QKV + 10 * HEADS * 256 ** 3, moved=16 << 20, limit=40,
    )(wide_at, block_t, grad_t, *weights)
    returned = exchange(through)

    packed_mate = across_cores(send)
    leave = product("leave", z_at, block_t, block_mate, keep, packed_mate, WIDE, WIDE, DUE)
    came = [along_plane(part, *step) for part, step in zip(leave, STEPS)]
    stay = product(
        "stay", after(z_at, leave[0]), block_t, block_mate, keep, packed_mate, 0, WIDE, [(index,) for index in range(Z)]
    )
    hidden_grad = plus(after(pair_grad, *stay, came[0], came[1]), returned)
    hidden_mine = lax.dynamic_slice(hidden_grad, (0, proj_at[0]), (P_SIZE, PW))
    hidden_mate = across_cores(lax.dynamic_slice(hidden_grad, (0, proj_at[1]), (P_SIZE, PW)))
    (proj_part,) = product(
        "proj_part", 0 * z_at, spatial_out, spatial_mate, hidden_mine, hidden_mate, 0, PW,
        [tuple(range(Z))]
    )
    arrived = {}
    for part, share in zip(came, DUE):
        for place, index in enumerate(share):
            arrived[index] = part[place * UNIT:(place + 1) * UNIT]
    proj_sum = lax.psum_scatter(proj_part, "z", scatter_dimension=0, tiled=True)
    first = plus(stay[4], arrived[4]), plus(stay[5], arrived[5])
    ahead = along_z(first[0], 1)
    behind = along_z(first[1], -1)
    spatial_grad = call(
        spatial_kernel, "spatial", shape(P_SIZE, QKV), [SMEM] + [VMEM] * 4, VMEM, [pltpu.VMEM((P_SIZE, D), BF)],
        flops=2 * P_SIZE * D * D + 10 * HEADS * 256 ** 3, moved=8 << 20,
    )(proj_at, spatial_qkv, hidden_grad, proj, proj_mate)
    for up, down in ((3, 6), (2, 7)):
        ahead, behind = lax.optimization_barrier((
            plus(stay[up], arrived[up], ahead), plus(stay[down], arrived[down], behind),
            proj_part if up == 3 else spatial_grad,
        ))[:2]
        ahead = along_z(ahead, 1)
        behind = along_z(behind, -1)
    ahead = along_z(after(plus(stay[1], arrived[1], ahead), behind), 1)
    weight_sum = plus(stay[0], arrived[0], ahead, behind)

    both = jnp.concatenate([weight_sum, proj_sum], axis=1)
    here = lax.dynamic_slice(both, (ROWS * y_lo, 0), (ROWS, WIDE + PW))
    there = lax.dynamic_slice(both, (ROWS * (1 - y_lo), 0), (ROWS, WIDE + PW))
    total = plus(here, along_plane(there, 1, 1), along_plane(there, -1, -1), along_plane(here, 0, 2))
    total = plus(total, along_plane(total, 2, 0))
    beside = lax.ppermute(total, "x", [(0, 1), (1, 0), (2, 3), (3, 2)])
    weight_sums = jnp.concatenate([total[:, :WIDE], beside[:, :WIDE]], axis=1)
    proj_sums = plus(total[:, WIDE:], beside[:, WIDE:])
    weight_grad, proj_grad = call(
        finish_kernel, "finish", [shape(ROWS, QKV), shape(ROWS, D)], [SMEM] * 2 + [VMEM] * 4, [VMEM] * 2, moved=2 << 20,
    )(wide_at, proj_at, weight_sums, across_cores(weight_sums), proj_sums, across_cores(proj_sums))
    return (
        spatial_grad.reshape(1, P_SIZE, QKV),
        hidden_grad.reshape(1, P_SIZE, D),
        proj_grad,
        weight_grad,
    )


def solution(mesh):
    fine = Mesh(mesh.devices.reshape(8, 2, 2, 4, 2), ("z", "yl", "yh", "x", "c"))
    tokens = P(("yh", "x", "c"), ("z", "yl"), None)
    rows = P(("z", "yl"), None)
    return jax.shard_map(
        per_device,
        mesh=fine,
        in_specs=(tokens, tokens, tokens, tokens, rows, rows),
        out_specs=(tokens, tokens, rows, rows),
        check_vma=False,
    )
```
